32 devices in a mesh: dom: 4 (over y, x), brick: 8 (over z, core).
Axes of the slice: x: 2, y: 2, z: 4, core: 2. Of those that a mesh axis runs over, the one named last changes fastest.
Arguments:
- positions: float32 [3, 2048, 128], P(None, ('dom', 'brick')), may hold values from 0 to 1
- direction: float32 [3, 2048, 128], P(None, ('dom', 'brick')), may hold values from -6 to 6
- pair_local: int32 [8192], P(('dom', 'brick')), may hold values from 0 to 63
- pair_peer: int32 [8192, 1], P(('dom', 'brick')), may hold values from 0 to 31; in each aligned block of 256 rows (0 to 255, 256 to 511, ...) at most 16 rows name the same one
- pair_remote: int32 [8192], P(('dom', 'brick')), may hold values from 0 to 63
- pair_mask: int32 [8192, 128], P(('dom', 'brick')), may hold values 0 or 1
Outputs:
- gradient: float32 [3, 2048, 128], P(None, ('dom', 'brick'))
- hess_dir: float32 [3, 2048, 128], P(None, ('dom', 'brick'))
The draws below stay inside these ranges and needn't reach their ends.
Inputs may be any that keep to these rules, and one draw needn't show every extreme that they name: `pair_peer`: among the 256 rows of one device no device is named more than 16 times.
All inputs are finite; a program needn't handle non-finite values. No bound on the sum of `pair_mask` on one device may be relied on, other than what follows from the above.
Results may differ from the reference program's by a relative error of at most 0.0003.
Values sent between devices are 32-bit elements; how exact they have to be, the bound alone decides.
No kernel may reach another device: no remote copies, remote signals or barrier semaphores. Data moves between devices by JAX's collectives and lax.ppermute only.
A program may use at most 64 MiB of HBM per device.

```python
import math
import jax
import jax.numpy as jnp
import numpy as np
from jax import lax

BS = 128
PAIRS_DEV = 256
BLK_DEV = 64
CAP = 16
BLOCKS = 2048
PAIRS = 8192
DEVICES = 32


def with_ends(drawn, rng, smallest, high):
    index_at = [jax.random.randint(jax.random.fold_in(rng, axis), (), 0, length) for axis, length in enumerate(drawn.shape)]
    main_axis = drawn.shape.index(max(drawn.shape))
    beside = index_at[:main_axis] + [(index_at[main_axis] + 1) % drawn.shape[main_axis]] + index_at[main_axis + 1:]
    return drawn.at[tuple(index_at)].set(smallest).at[tuple(beside)].set(high)


def level_of(rng, shape, shards, smallest, top_value):
    def one(axis_at, blocks):
        heights = jax.random.uniform(jax.random.fold_in(jax.random.fold_in(rng, 6), axis_at), (blocks,), jnp.float32, smallest / len(shards), top_value / len(shards))
        return jnp.repeat(jnp.exp(heights), shape[axis_at] // blocks).reshape((-1,) + (1,) * (len(shape) - axis_at - 1))

    level = one(*shards[0])
    for cut in shards[1:]:
        level = level * one(*cut)
    return level


def routed_block(key, own, number, rows, count, top, limit, slope):
    order = jax.random.permutation(key, count)
    crowded, usual = portions_of(count, rows * top, limit, slope, True), portions_of(count, rows * top, limit, slope, False)
    places = jnp.arange(count)

    def named(sizes, rotation):
        used = int((sizes > 0).sum())
        fixed = max(1, used // 4)
        moved = fixed + (places - fixed + rotation * (used - fixed)) % max(1, count - fixed)
        return jnp.zeros((count,), jnp.int32).at[order[jnp.where(places < fixed, places, moved)]].set(jnp.asarray(sizes, jnp.int32))

    sizes = jnp.where(number % 4 == 0, named(crowded, number // 4), named(usual, number - number // 4 - 1))
    mixed = jax.random.permutation(jax.random.fold_in(own, 3), count)
    giver, taker = mixed[0:count // 2 * 2:2], mixed[1:count // 2 * 2:2]
    margin = jnp.minimum(sizes[giver] - 1, limit - sizes[taker]) // 2
    margin = jnp.where((giver == order[0]) | (taker == order[0]) | (sizes[taker] == 0), 0, jnp.maximum(margin, 0))
    moved = jax.random.randint(jax.random.fold_in(own, 4), (count // 2,), 0, 1 << 20) % (margin + 1)
    sizes = sizes.at[giver].add(-moved).at[taker].add(moved)
    members = jnp.searchsorted(jnp.cumsum(sizes), jnp.arange(rows * top), side="right").astype(jnp.int32)
    table = members.reshape(top, rows).T
    table = table[jax.random.permutation(jax.random.fold_in(own, 1), rows)]
    rotation = jax.random.randint(jax.random.fold_in(own, 2), (rows, 1), 0, top)
    return jnp.take_along_axis(table, (jnp.arange(top)[None, :] + rotation) % top, axis=1)


def portions_of(amount, total, reach, lean, full):
    portions = [(1 << 20) // math.isqrt(grade ** lean) + 1 for grade in range(1, amount + 1)]
    largest = reach if full else min(reach, max(-(-total // amount), total * portions[0] // sum(portions)))
    least = 1 if total - largest >= amount - 1 else 0
    counts, spare = [largest] + [least] * (amount - 1), total - largest - least * (amount - 1)
    while spare > 0:
        movable = [i for i in range(1, amount) if counts[i] < largest] or [i for i in range(1, amount) if counts[i] < reach]
        whole, budget = sum([portions[i] for i in movable]), spare
        for i in movable:
            addition = min(reach - counts[i], max(1, budget * portions[i] // whole), spare)
            counts[i] = counts[i] + addition
            spare = spare - addition
    return np.array(counts)


def normal_values(key, shape, scale, most, pieces=(), dtype=jnp.bfloat16):
    drawn = jax.random.normal(key, shape, jnp.float32) * scale
    if len(pieces) > 0:
        drawn = level_of(key, shape, pieces, -0.22, 0.18) * drawn
    return jnp.clip(drawn, min=-most, max=most).astype(dtype)


def setup_inputs(seed: int = 0) -> dict:
    seeds = jax.random.split(jax.random.key(seed), 7)
    positions = jnp.clip(1.0 * jax.random.uniform(seeds[0], (3, BLOCKS, BS), jnp.float32) ** level_of(seeds[0], (3, BLOCKS, BS), ((1, 32),), -0.2, 0.2), 0.0, 1.0)
    direction = normal_values(seeds[1], (3, BLOCKS, BS), 1.0, 6.0, ((1, 32),), jnp.float32)
    pair_local = with_ends(jax.random.randint(seeds[2], (PAIRS,), 0, BLK_DEV), jax.random.fold_in(seeds[2], 1), 0, BLK_DEV - 1).astype(jnp.int32)
    pair_peer_keys = jax.random.split(jax.random.fold_in(seeds[3], 1), PAIRS // PAIRS_DEV)
    pair_peer_turns = jax.random.permutation(jax.random.fold_in(seeds[3], 3), PAIRS // PAIRS_DEV)
    pair_peer = jax.vmap(lambda own, number: routed_block(jax.random.fold_in(seeds[3], 2), own, number, PAIRS_DEV, DEVICES, 1, CAP, 2))(pair_peer_keys, pair_peer_turns).reshape((PAIRS, 1))
    pair_remote = with_ends(jax.random.randint(seeds[4], (PAIRS,), 0, BLK_DEV), jax.random.fold_in(seeds[4], 1), 0, BLK_DEV - 1).astype(jnp.int32)
    pair_mask = with_ends((jax.random.randint(seeds[5], (PAIRS, BS), 0, 4) < 3).astype(jnp.int32), jax.random.fold_in(seeds[5], 1), 0, 1)
    return {"positions": positions, "direction": direction, "pair_local": pair_local, "pair_peer": pair_peer, "pair_remote": pair_remote, "pair_mask": pair_mask}


thick = 0.1
kappa = 0.005


def tile_terms(own, partner, mask):
    r = own[:3, :, :, None] - partner[:3, :, None, :]
    s = jnp.sum(r * r, axis=0) + thick
    gap = s - 1.0
    logs = jnp.log(s)
    first = -2.0 * gap * logs - gap * gap / s
    second = -2.0 * logs - 4.0 * gap / s + gap * gap / (s * s)
    live = (s < 1.0) & (mask[:, :, None] > 0)
    w = own[3:, :, :, None] - partner[3:, :, None, :]
    c_one = jnp.where(live, 2.0 * kappa * first, 0.0)
    c_two = jnp.where(live, 4.0 * kappa * second * jnp.sum(r * w, axis=0), 0.0)
    grad_part = c_one * r
    hv_part = c_two * r + c_one * w
    both = jnp.concatenate([grad_part, hv_part], axis=0)
    return jnp.sum(both, axis=3), -jnp.sum(both, axis=2)


def reference(positions, direction, pair_local, pair_peer, pair_remote, pair_mask):
    total = pair_local.shape[0]
    owner = (jnp.arange(total) // PAIRS_DEV).astype(jnp.int32)
    left_block = (owner * BLK_DEV + pair_local).astype(jnp.int32)
    block_b = (pair_peer[:, 0] * BLK_DEV + pair_remote).astype(jnp.int32)
    data = jnp.concatenate([positions, direction], axis=0)
    batch = 64
    steps = total // batch
    index_a = left_block.reshape(steps, batch)
    index_b = block_b.reshape(steps, batch)
    masks = pair_mask.reshape(steps, batch, BS)

    def advance(acc, items):
        ia, ib, mk = items
        own = jnp.take(data, ia, axis=1)
        partner = jnp.take(data, ib, axis=1)
        left_term, right_term = tile_terms(own, partner, mk)
        acc = acc.at[:, ia].add(left_term)
        acc = acc.at[:, ib].add(right_term)
        return acc, None

    start = jnp.zeros(data.shape, jnp.float32)
    acc, _ = lax.scan(advance, start, (index_a, index_b, masks))
    return acc[:3], acc[3:]
```

```python
import functools

import jax
import jax.numpy as jnp
import numpy as np
from jax import lax
from jax.experimental import pallas as pl
from jax.experimental.pallas import tpu as pltpu
from jax.sharding import PartitionSpec as P

AXES = ("dom", "brick")
F32, BF16, I32 = jnp.float32, jnp.bfloat16, jnp.int32
GROUP = 8
LOG_SCALE = 2.0 * 0.6931471805599453
SMEM = pl.BlockSpec(memory_space=pltpu.SMEM)
VMEM = pl.BlockSpec(memory_space=pltpu.VMEM)


def iota(shape, dim):
    return lax.broadcasted_iota(I32, shape, dim)


def params(mib):
    return pltpu.CompilerParams(vmem_limit_bytes=mib << 20)


def pack_kernel(ndev, slots, stride, pos_ref, dir_ref, peer_ref, local_ref, remote_ref, mask_ref, data_ref, send_ref, mine_ref):
    nblocks = pos_ref.shape[1]
    npairs = peer_ref.shape[1]
    for c in range(3):
        data_ref[pl.ds(c, nblocks, stride=6), :] = pos_ref[c]
        data_ref[pl.ds(3 + c, nblocks, stride=6), :] = dir_ref[c]
    square = (npairs, npairs)
    rows, cols = iota(square, 0), iota(square, 1)

    def column(row):
        return jnp.sum(jnp.where(rows == cols, row, 0), axis=1, keepdims=True)

    peer = peer_ref[...]
    peer_col = column(peer)
    same = peer_col == peer
    rank = jnp.sum(jnp.where(same & (rows < cols), 1, 0), axis=0, keepdims=True)
    rank_col = jnp.sum(jnp.where(same & (cols < rows), 1, 0), axis=1, keepdims=True)
    local_col, remote_col = column(local_ref[...]), column(remote_ref[...])
    lane = iota((npairs, 128), 1)
    part, place = lane // slots, lane % slots
    pair = iota((npairs, 128), 0)
    value = jnp.where(part == 0, local_col, jnp.where(part == 1, remote_col, jnp.where(part == 2, pair, jnp.where(part == 3, 1, 0))))
    numbers = jnp.where(place == rank_col, value, 0).astype(F32).astype(BF16)
    mask = mask_ref[...].astype(F32).astype(BF16)
    slot = iota((ndev * stride, npairs), 0)
    hot = jnp.where(slot == peer * stride + rank, 1.0, 0.0).astype(BF16)
    hot_numbers = jnp.where(slot == peer * stride + slots, 1.0, 0.0).astype(BF16)
    send_ref[...] = jnp.dot(hot, mask, preferred_element_type=F32) + jnp.dot(hot_numbers, numbers, preferred_element_type=F32)
    hot_peer = jnp.where(iota((ndev, npairs), 0) == peer, 1.0, 0.0).astype(BF16)
    mine_ref[...] = jnp.dot(hot_peer, numbers, preferred_element_type=F32)


def pack(ndev, slots, stride, positions, direction, peer, local, remote, mask):
    nblocks = positions.shape[1]
    return pl.pallas_call(
        functools.partial(pack_kernel, ndev, slots, stride),
        out_shape=(
            jax.ShapeDtypeStruct((nblocks * 6, 128), F32),
            jax.ShapeDtypeStruct((ndev * stride, 128), F32),
            jax.ShapeDtypeStruct((ndev, 128), F32),
        ),
        in_specs=[VMEM] * 6,
        out_specs=(VMEM,) * 3,
        compiler_params=params(16),
        name="pack",
    )(positions, direction, peer, local, remote, mask)


def split(v):
    h = v.astype(BF16).astype(F32)
    e = v - h
    m = e.astype(BF16).astype(F32)
    return h, m, e - m


def products(d, h, m, row):
    both = h + m
    return both * jnp.where(row < 3, both, pltpu.roll(both, 3, 0))


def other_features(d, row):
    h, m, l = split(d)
    vh, vm, vl = split(products(d, h, m, row))
    hm = jnp.concatenate([h, m], 0).astype(BF16)
    vhm = jnp.concatenate([vh, vm], 0).astype(BF16)
    vlo = jnp.concatenate([vl, jnp.ones_like(d)], 0).astype(BF16)
    first = jnp.where(row < 6, h, jnp.where(row == 6, 1.0, pltpu.roll(l, 7, 0)))
    second = jnp.where(row < 6, m, pltpu.roll(l, 5, 0))
    return jnp.concatenate([hm, hm, vhm, vlo], 0), jnp.concatenate([first, second], 0)


def own_features(d, row):
    d = jnp.where(row < 6, d, 0.0)
    h, m, _ = split(d)
    v = products(d, h, m, row)
    total = v + pltpu.roll(v, 7, 0) + pltpu.roll(v, 6, 0)

    def parts(one_row):
        ph, pm, pl_ = split(jnp.broadcast_to(one_row, d.shape))
        return jnp.where(row == 0, ph, jnp.where(row == 1, pm, jnp.where(row == 2, pl_, 0.0)))

    def cross(a):
        return jnp.where(row < 3, -pltpu.roll(a, 5, 0), jnp.where(row < 6, -pltpu.roll(a, 3, 0), 0.0))

    hs, ms = jnp.where(row < 3, -2.0 * h, 0.0), jnp.where(row < 3, -2.0 * m, 0.0)
    hq, mq = cross(h), cross(m)
    low = jnp.where(row < 3, 1.0, 0.0)
    high = jnp.where((row >= 3) & (row < 6), 1.0, 0.0)
    for_s = jnp.concatenate([hs, ms, ms, hs, low, low, low, parts(total[0:1] + 0.1)], 0)
    for_q = jnp.concatenate([hq, mq, mq, hq, high, high, high, parts(total[3:4])], 0)
    return jnp.concatenate([for_s, for_q], 1).astype(BF16)


def plan_kernel(
    slots, stride, nlists, capacity, me_ref, table_ref, mine_ref, came_ref, mask_ref, data_ref,
    list_ref, count_ref, masks_ref, own_ref, code_vmem, code_smem, sem,
):
    ndev = mine_ref.shape[0]
    npairs = mask_ref.shape[0]
    nblocks = own_ref.shape[0]
    lane = iota((ndev, 128), 1)
    peer = iota((ndev, 128), 0)
    rel = iota((ndev, ndev), 0) ^ me_ref[0]
    entry = jnp.sum(jnp.where(iota((ndev, ndev), 1) == rel, table_ref[...], 0), axis=1, keepdims=True)
    which, unit = entry // 256, entry % 256

    def codes(numbers, mine):
        numbers = numbers.astype(I32)
        first = numbers
        second = pltpu.roll(numbers, 128 - slots, 1)
        third = pltpu.roll(numbers, 128 - 2 * slots, 1)
        used = jnp.where((lane >= 3 * slots) & (lane < 4 * slots), numbers, 0)
        count = jnp.sum(used, axis=1, keepdims=True)
        if mine:
            own, other, mask = first, second, third
        else:
            own, other, mask = second, first, npairs + peer * stride + lane
        code = (unit * nblocks + other) + own * (1 << 14) + mask * (1 << 20)
        return jnp.where(lane < slots, code, jnp.where(lane == slots, count, which))

    code_vmem[0:ndev, :] = codes(mine_ref[...], True)
    code_vmem[ndev:, :] = codes(came_ref[pl.ds(slots, ndev, stride=stride), :], False)
    copy = pltpu.make_async_copy(code_vmem, code_smem, sem)
    copy.start()
    masks_ref[0:npairs, :] = mask_ref[...].astype(F32)
    masks_ref[npairs : npairs + ndev * stride, :] = came_ref[...]
    masks_ref[npairs + ndev * stride :, :] = jnp.zeros((8, 128), F32)
    row = iota((8, 128), 0)

    def feature(i, _):
        for u in range(4):
            b = i * 4 + u
            start = jnp.minimum(b * 6, nblocks * 6 - 8)
            d = data_ref[pl.ds(start, 8), :]
            d = jnp.where(b == nblocks - 1, pltpu.roll(d, 6, 0), d)
            own_ref[b] = own_features(d, row)
        return 0

    lax.fori_loop(0, nblocks // 4, feature, 0)
    copy.wait()
    for k in range(nlists):
        count_ref[k] = 0

    def fill(p, _):
        k = code_smem[p, slots + 1]
        at = count_ref[k]
        for r in range(slots):
            list_ref[k * capacity + at + r] = code_smem[p, r]
        count_ref[k] = at + code_smem[p, slots]
        return 0

    lax.fori_loop(0, 2 * ndev, fill, 0)
    for k in range(nlists):
        at = count_ref[k]
        for r in range(GROUP):
            list_ref[k * capacity + at + r] = (npairs + ndev * stride) * (1 << 20)


def plan(slots, stride, nlists, me, table, mine, came, mask, data):
    ndev, npairs, nblocks = mine.shape[0], mask.shape[0], data.shape[0] // 6
    capacity = npairs + ndev * slots + slots + GROUP
    out = pl.pallas_call(
        functools.partial(plan_kernel, slots, stride, nlists, capacity),
        out_shape=(
            jax.ShapeDtypeStruct((nlists * capacity,), I32),
            jax.ShapeDtypeStruct((nlists,), I32),
            jax.ShapeDtypeStruct((npairs + ndev * stride + 8, 128), F32),
            jax.ShapeDtypeStruct((nblocks, 64, 256), BF16),
        ),
        in_specs=[SMEM] + [VMEM] * 5,
        out_specs=(SMEM, SMEM, VMEM, VMEM),
        scratch_shapes=[pltpu.VMEM((2 * ndev, 128), I32), pltpu.SMEM((2 * ndev, 128), I32), pltpu.SemaphoreType.DMA],
        compiler_params=params(16),
        name="plan",
    )(me, table, mine, came, mask, data)
    return capacity, out


def halves(c):
    h = c.astype(BF16)
    return h, (c - h.astype(F32)).astype(BF16)


def prepare(codes, block_ref, masks_ref, npairs, k_ref, f_ref):
    row = iota((8, 128), 0)
    for g, code in enumerate(codes):
        d = block_ref[pl.ds((code & 0x3FFF) * 6, 8), :]
        left, sums = other_features(d, row)
        place = code >> 20
        mask = jnp.where(place < npairs, 1.0, masks_ref[pl.ds(place, 1), :])
        f_ref[g] = (sums * mask).astype(BF16)
        k_ref[g] = left.T


def accumulate(codes, own_ref, masks_ref, npairs, acc_ref, k_ref, f_ref):
    outs = []
    for g, code in enumerate(codes):
        own = (code >> 14) & 63
        both = jnp.dot(k_ref[g], own_ref[own], preferred_element_type=F32)
        s = jnp.minimum(both[:, :128], 1.0)
        gap = s - 1.0
        log = LOG_SCALE * jnp.log2(s)
        ratio = gap * pl.reciprocal(s, approx=True)
        one = gap * (log + ratio)
        two = ((ratio - 4.0) * ratio - log) * both[:, 128:]
        one_h, one_l = halves(one)
        two_h, two_l = halves(two)
        weights = jnp.concatenate([jnp.concatenate([one_h, two_h], 1), jnp.concatenate([one_l, two_l], 1)], 0)
        f = f_ref[g]
        out = jnp.dot(jnp.concatenate([f, f], 1), weights, preferred_element_type=F32)
        place = code >> 20
        mask = jnp.where(place < npairs, masks_ref[pl.ds(place, 1), :], 1.0)
        outs.append((own, out * jnp.concatenate([mask, mask], 1)))
    for own, out in outs:
        acc_ref[own] += out


def finish(data_ref, acc_ref, grad_ref, hess_ref):
    nblocks = acc_ref.shape[0]
    row = iota((8, 128), 0)

    def block(b, _):
        start = jnp.minimum(b * 6, nblocks * 6 - 8)
        d = data_ref[pl.ds(start, 8), :]
        d = jnp.where(b == nblocks - 1, pltpu.roll(d, 6, 0), d)
        acc = acc_ref[b]

        def sums(a):
            first, second = a[0:8], a[8:16]
            total = first + second
            low = jnp.where(row == 0, pltpu.roll(first, 1, 0), jnp.where(row < 3, pltpu.roll(second, 3, 0), 0.0))
            return first[6:7], total + low

        n_one, y_one = sums(acc[:, :128] * -0.01)
        n_two, y_two = sums(acc[:, 128:] * 0.02)
        a = d * n_one - y_one
        c = d * n_two - y_two + pltpu.roll(a, 5, 0)
        for k in range(3):
            grad_ref[k, pl.ds(b, 1), :] = a[k : k + 1]
            hess_ref[k, pl.ds(b, 1), :] = c[k : k + 1]
        return 0

    lax.fori_loop(0, nblocks, block, 0)


def task_kernel(lists, capacity, npairs, first, last, *refs):
    list_ref, count_ref, masks_ref, own_ref, data_ref = refs[:5]
    blocks, refs = refs[5 : 5 + len(lists)], refs[5 + len(lists) :]
    if not first:
        before_ref, refs = refs[0], refs[1:]
    if last:
        grad_ref, hess_ref, acc_ref, k_ref, f_ref = refs
    else:
        acc_ref, k_ref, f_ref = refs
    if first:
        acc_ref[...] = jnp.zeros_like(acc_ref)
    else:
        acc_ref[...] = before_ref[...]
    for k, block_ref in zip(lists, blocks):
        count = count_ref[k]
        groups = (count + GROUP - 1) // GROUP

        def codes(i, k=k):
            return [list_ref[k * capacity + i * GROUP + g] for g in range(GROUP)]

        @pl.when(groups > 0)
        def _(block_ref=block_ref, codes=codes, groups=groups):
            prepare(codes(0), block_ref, masks_ref, npairs, k_ref, f_ref)

            def step(i, _):
                accumulate(codes(i), own_ref, masks_ref, npairs, acc_ref, k_ref, f_ref)
                prepare(codes(jnp.minimum(i + 1, groups - 1)), block_ref, masks_ref, npairs, k_ref, f_ref)
                return 0

            lax.fori_loop(0, groups, step, 0)

    if last:
        finish(data_ref, acc_ref, grad_ref, hess_ref)


def tasks(lists, capacity, npairs, list_, count, masks, own, data, blocks, before, last):
    nblocks = own.shape[0]
    acc = jax.ShapeDtypeStruct((nblocks, 16, 256), F32)
    out = jax.ShapeDtypeStruct((3, nblocks, 128), F32)
    first = before is None
    scratch = [pltpu.VMEM((GROUP, 128, 64), BF16), pltpu.VMEM((GROUP, 16, 128), BF16)]
    if last:
        scratch = [pltpu.VMEM(acc.shape, F32)] + scratch
    args = [list_, count, masks, own, data, *blocks] + ([] if first else [before])
    size = sum(b.size for b in blocks) * 4
    return pl.pallas_call(
        functools.partial(task_kernel, lists, capacity, npairs, first, last),
        out_shape=(out, out) if last else acc,
        in_specs=[SMEM, SMEM] + [VMEM] * (len(args) - 2),
        out_specs=(VMEM, VMEM) if last else VMEM,
        scratch_shapes=scratch,
        compiler_params=params(24),
        cost_estimate=pl.CostEstimate(flops=size * 2000, bytes_accessed=size * 3, transcendentals=0),
        name="tasks",
    )(*args)


class Piece:
    def __init__(self, tags, array):
        self.tags, self.array = list(tags), array

    def cut(self, start, stop):
        rows = self.array.shape[0] // len(self.tags)
        return Piece(self.tags[start:stop], self.array[start * rows : stop * rows])


def join(pieces):
    if len(pieces) == 1:
        return pieces[0]
    return Piece(sum([p.tags for p in pieces], []), jnp.concatenate([p.array for p in pieces], axis=0))


def swap(piece, bit, ndev):
    pairs = [(i, i ^ (1 << bit)) for i in range(ndev)]
    return Piece([t ^ (1 << bit) for t in piece.tags], lax.ppermute(piece.array, AXES, pairs))


def exchange(data, ndev):
    bits = ndev.bit_length() - 1
    x, y = bits - 2, bits - 1
    column = list(range(bits - 3, 0, -1))
    own = Piece([0], data)
    held, part, phases = own, own, []
    over_x, over_y = [], []
    for bit in column:
        new = swap(held, bit, ndev)
        px, py = swap(part, x, ndev), swap(part, y, ndev)
        over_x.append(px)
        over_y.append(py)
        phases.append([part, px, py])
        held, part = join([held, new]), new
    earlier_x, earlier_y = join(over_x), join(over_y)
    half = len(earlier_x.tags) // 2
    ax = swap(join([part, earlier_y.cut(0, half)]), x, ndev)
    ay = swap(join([part, earlier_x.cut(half, 2 * half)]), y, ndev)
    phases.append([part, ax, ay])
    size = len(part.tags)
    bx = swap(ay.cut(0, size // 2), x, ndev)
    by = swap(ax.cut(size // 2, size), y, ndev)
    phases.append([bx, by])
    return phases


def on_device(positions, direction, pair_local, pair_peer, pair_remote, pair_mask):
    npairs = pair_local.shape[0]
    nblocks = positions.shape[1]
    ndev = lax.axis_size(AXES)
    me = lax.axis_index(AXES).astype(I32)
    slots = max(2, 2 * npairs // ndev)
    stride = -(-(slots + 1) // 8) * 8
    peer, local, remote = (a.reshape(1, npairs) for a in (pair_peer, pair_local, pair_remote))
    data, send, mine = pack(ndev, slots, stride, positions, direction, peer, local, remote, pair_mask)
    came = lax.all_to_all(send, AXES, split_axis=0, concat_axis=0, tiled=True)

    phases = [join(p) for p in exchange(data, ndev)]
    tail = jnp.zeros((8, 128), F32)
    table = np.zeros((1, ndev), np.int32)
    blocks = []
    for k, piece in enumerate(phases):
        near = Piece(piece.tags, jnp.concatenate([piece.array, tail], axis=0))
        far = swap(Piece(piece.tags, near.array), 0, ndev)
        for which, p in ((2 * k, near), (2 * k + 1, far)):
            for unit, tag in enumerate(p.tags):
                table[0, tag] = which * 256 + unit
        blocks.append((near.array, far.array))
    nlists = 2 * len(phases)
    capacity, (list_, count, masks, own) = plan(
        slots, stride, nlists, me.reshape(1), jnp.asarray(table), mine, came, pair_mask, data
    )
    acc = None
    for k, pair in enumerate(blocks):
        last = k == len(blocks) - 1
        acc = tasks((2 * k, 2 * k + 1), capacity, npairs, list_, count, masks, own, data, pair, acc, last)
    return acc


def solution(mesh):
    blocked = P(None, AXES, None)
    in_specs = (blocked, blocked, P(AXES), P(AXES, None), P(AXES), P(AXES, None))
    return jax.shard_map(on_device, mesh=mesh, in_specs=in_specs, out_specs=(blocked, blocked), check_vma=False)
```

```python
import functools

import jax
import jax.numpy as jnp
import numpy as np
from jax import lax
from jax.experimental import pallas as pl
from jax.experimental.pallas import tpu as pltpu
from jax.sharding import PartitionSpec as P

AXES = ("dom", "brick")
F32, BF16, I32 = jnp.float32, jnp.bfloat16, jnp.int32
GROUP = 8
LOG_SCALE = 2.0 * 0.6931471805599453
SMEM = pl.BlockSpec(memory_space=pltpu.SMEM)
VMEM = pl.BlockSpec(memory_space=pltpu.VMEM)
ANY = pl.BlockSpec(memory_space=pl.ANY)


def iota(shape, dim):
    return lax.broadcasted_iota(I32, shape, dim)


def params(mib):
    return pltpu.CompilerParams(vmem_limit_bytes=mib << 20)


def fetch(pairs, sems):
    copies = [pltpu.make_async_copy(src, dst, sems.at[i]) for i, (src, dst) in enumerate(pairs)]
    for copy in copies:
        copy.start()
    for copy in copies:
        copy.wait()


def weave_kernel(pos_hbm, dir_hbm, data_ref, pos_ref, dir_ref, sems):
    fetch([(pos_hbm, pos_ref), (dir_hbm, dir_ref)], sems)
    nblocks = pos_ref.shape[1]
    for c in range(3):
        data_ref[pl.ds(c, nblocks, stride=6), :] = pos_ref[c]
        data_ref[pl.ds(3 + c, nblocks, stride=6), :] = dir_ref[c]


def weave(positions, direction):
    nblocks = positions.shape[1]
    whole = pltpu.VMEM(positions.shape, F32)
    return pl.pallas_call(
        weave_kernel,
        out_shape=jax.ShapeDtypeStruct((nblocks * 6, 128), F32),
        in_specs=[ANY] * 2,
        out_specs=VMEM,
        scratch_shapes=[whole, whole, pltpu.SemaphoreType.DMA((2,))],
        compiler_params=params(16),
        name="weave",
    )(positions, direction)


def pack_kernel(
    ndev, slots, stride, peer_hbm, local_hbm, remote_hbm, mask_hbm, data_hbm, send_ref, mine_ref,
    peer_ref, local_ref, remote_ref, mask_ref, sems,
):
    fetch([(peer_hbm, peer_ref), (local_hbm, local_ref), (remote_hbm, remote_ref), (mask_hbm, mask_ref)], sems)
    npairs = peer_ref.shape[1]
    square = (npairs, npairs)
    rows, cols = iota(square, 0), iota(square, 1)

    def column(row):
        return jnp.sum(jnp.where(rows == cols, row, 0), axis=1, keepdims=True)

    peer = peer_ref[...]
    peer_col = column(peer)
    same = peer_col == peer
    rank = jnp.sum(jnp.where(same & (rows < cols), 1, 0), axis=0, keepdims=True)
    rank_col = jnp.sum(jnp.where(same & (cols < rows), 1, 0), axis=1, keepdims=True)
    local_col, remote_col = column(local_ref[...]), column(remote_ref[...])
    lane = iota((npairs, 128), 1)
    part, place = lane // slots, lane % slots
    pair = iota((npairs, 128), 0)
    value = jnp.where(part == 0, local_col, jnp.where(part == 1, remote_col, jnp.where(part == 2, pair, jnp.where(part == 3, 1, 0))))
    numbers = jnp.where(place == rank_col, value, 0).astype(F32).astype(BF16)
    mask = mask_ref[...].astype(F32).astype(BF16)
    slot = iota((ndev * stride, npairs), 0)
    hot = jnp.where(slot == peer * stride + rank, 1.0, 0.0).astype(BF16)
    hot_numbers = jnp.where(slot == peer * stride + slots, 1.0, 0.0).astype(BF16)
    send_ref[...] = jnp.dot(hot, mask, preferred_element_type=F32) + jnp.dot(hot_numbers, numbers, preferred_element_type=F32)
    hot_peer = jnp.where(iota((ndev, npairs), 0) == peer, 1.0, 0.0).astype(BF16)
    mine_ref[...] = jnp.dot(hot_peer, numbers, preferred_element_type=F32)


def pack(ndev, slots, stride, peer, local, remote, mask, data):
    row = pltpu.VMEM(peer.shape, I32)
    return pl.pallas_call(
        functools.partial(pack_kernel, ndev, slots, stride),
        out_shape=(jax.ShapeDtypeStruct((ndev * stride, 128), F32), jax.ShapeDtypeStruct((ndev, 128), F32)),
        in_specs=[ANY] * 5,
        out_specs=(VMEM,) * 2,
        scratch_shapes=[row, row, row, pltpu.VMEM(mask.shape, I32), pltpu.SemaphoreType.DMA((4,))],
        compiler_params=params(16),
        name="pack",
    )(peer, local, remote, mask, data)


def split(v):
    h = v.astype(BF16).astype(F32)
    e = v - h
    m = e.astype(BF16).astype(F32)
    return h, m, e - m


def products(d, h, m, row):
    both = h + m
    return both * jnp.where(row < 3, both, pltpu.roll(both, 3, 0))


def other_features(d, row):
    h, m, l = split(d)
    vh, vm, vl = split(products(d, h, m, row))
    hm = jnp.concatenate([h, m], 0).astype(BF16)
    vhm = jnp.concatenate([vh, vm], 0).astype(BF16)
    vlo = jnp.concatenate([vl, jnp.ones_like(d)], 0).astype(BF16)
    first = jnp.where(row < 6, h, jnp.where(row == 6, 1.0, pltpu.roll(l, 7, 0)))
    second = jnp.where(row < 6, m, pltpu.roll(l, 5, 0))
    return jnp.concatenate([hm, hm, vhm, vlo], 0), jnp.concatenate([first, second], 0)


def own_features(d, row):
    d = jnp.where(row < 6, d, 0.0)
    h, m, _ = split(d)
    v = products(d, h, m, row)
    total = v + pltpu.roll(v, 7, 0) + pltpu.roll(v, 6, 0)

    def parts(one_row):
        ph, pm, pl_ = split(jnp.broadcast_to(one_row, d.shape))
        return jnp.where(row == 0, ph, jnp.where(row == 1, pm, jnp.where(row == 2, pl_, 0.0)))

    def cross(a):
        return jnp.where(row < 3, -pltpu.roll(a, 5, 0), jnp.where(row < 6, -pltpu.roll(a, 3, 0), 0.0))

    hs, ms = jnp.where(row < 3, -2.0 * h, 0.0), jnp.where(row < 3, -2.0 * m, 0.0)
    hq, mq = cross(h), cross(m)
    low = jnp.where(row < 3, 1.0, 0.0)
    high = jnp.where((row >= 3) & (row < 6), 1.0, 0.0)
    for_s = jnp.concatenate([hs, ms, ms, hs, low, low, low, parts(total[0:1] + 0.1)], 0)
    for_q = jnp.concatenate([hq, mq, mq, hq, high, high, high, parts(total[3:4])], 0)
    return jnp.concatenate([for_s, for_q], 1).astype(BF16)


def plan_kernel(
    slots, stride, nlists, capacity, me_ref, table_ref, mine_ref, came_ref, mask_ref, data_ref,
    list_ref, count_ref, masks_ref, own_ref, code_vmem, code_smem, sem,
):
    ndev = mine_ref.shape[0]
    npairs = mask_ref.shape[0]
    nblocks = own_ref.shape[0]
    lane = iota((ndev, 128), 1)
    peer = iota((ndev, 128), 0)
    rel = iota((ndev, ndev), 0) ^ me_ref[0]
    entry = jnp.sum(jnp.where(iota((ndev, ndev), 1) == rel, table_ref[...], 0), axis=1, keepdims=True)
    which, unit = entry // 256, entry % 256

    def codes(numbers, mine):
        numbers = numbers.astype(I32)
        first = numbers
        second = pltpu.roll(numbers, 128 - slots, 1)
        third = pltpu.roll(numbers, 128 - 2 * slots, 1)
        used = jnp.where((lane >= 3 * slots) & (lane < 4 * slots), numbers, 0)
        count = jnp.sum(used, axis=1, keepdims=True)
        if mine:
            own, other, mask = first, second, third
        else:
            own, other, mask = second, first, npairs + peer * stride + lane
        code = (unit * nblocks + other) + own * (1 << 14) + mask * (1 << 20)
        return jnp.where(lane < slots, code, jnp.where(lane == slots, count, which))

    code_vmem[0:ndev, :] = codes(mine_ref[...], True)
    code_vmem[ndev:, :] = codes(came_ref[pl.ds(slots, ndev, stride=stride), :], False)
    copy = pltpu.make_async_copy(code_vmem, code_smem, sem)
    copy.start()
    masks_ref[0:npairs, :] = mask_ref[...].astype(F32)
    masks_ref[npairs : npairs + ndev * stride, :] = came_ref[...]
    masks_ref[npairs + ndev * stride :, :] = jnp.zeros((8, 128), F32)
    row = iota((8, 128), 0)

    def feature(i, _):
        for u in range(4):
            b = i * 4 + u
            start = jnp.minimum(b * 6, nblocks * 6 - 8)
            d = data_ref[pl.ds(start, 8), :]
            d = jnp.where(b == nblocks - 1, pltpu.roll(d, 6, 0), d)
            own_ref[b] = own_features(d, row)
        return 0

    lax.fori_loop(0, nblocks // 4, feature, 0)
    copy.wait()
    for k in range(nlists):
        count_ref[k] = 0

    def fill(p, _):
        k = code_smem[p, slots + 1]
        at = count_ref[k]
        for r in range(slots):
            list_ref[k * capacity + at + r] = code_smem[p, r]
        count_ref[k] = at + code_smem[p, slots]
        return 0

    lax.fori_loop(0, 2 * ndev, fill, 0)
    for k in range(nlists):
        at = count_ref[k]
        for r in range(GROUP):
            list_ref[k * capacity + at + r] = (npairs + ndev * stride) * (1 << 20)


def plan(slots, stride, nlists, me, table, mine, came, mask, data):
    ndev, npairs, nblocks = mine.shape[0], mask.shape[0], data.shape[0] // 6
    capacity = npairs + ndev * slots + slots + GROUP
    out = pl.pallas_call(
        functools.partial(plan_kernel, slots, stride, nlists, capacity),
        out_shape=(
            jax.ShapeDtypeStruct((nlists * capacity,), I32),
            jax.ShapeDtypeStruct((nlists,), I32),
            jax.ShapeDtypeStruct((npairs + ndev * stride + 8, 128), F32),
            jax.ShapeDtypeStruct((nblocks, 64, 256), BF16),
        ),
        in_specs=[SMEM] + [VMEM] * 5,
        out_specs=(SMEM, SMEM, VMEM, VMEM),
        scratch_shapes=[pltpu.VMEM((2 * ndev, 128), I32), pltpu.SMEM((2 * ndev, 128), I32), pltpu.SemaphoreType.DMA],
        compiler_params=params(16),
        name="plan",
    )(me, table, mine, came, mask, data)
    return capacity, out


def halves(c):
    h = c.astype(BF16)
    return h, (c - h.astype(F32)).astype(BF16)


def prepare(codes, block_ref, masks_ref, npairs, k_ref, f_ref):
    row = iota((8, 128), 0)
    for g, code in enumerate(codes):
        d = block_ref[pl.ds((code & 0x3FFF) * 6, 8), :]
        left, sums = other_features(d, row)
        place = code >> 20
        mask = jnp.where(place < npairs, 1.0, masks_ref[pl.ds(place, 1), :])
        f_ref[g] = (sums * mask).astype(BF16)
        k_ref[g] = left.T


def accumulate(codes, own_ref, masks_ref, npairs, acc_ref, k_ref, f_ref):
    outs = []
    for g, code in enumerate(codes):
        own = (code >> 14) & 63
        both = jnp.dot(k_ref[g], own_ref[own], preferred_element_type=F32)
        s = jnp.minimum(both[:, :128], 1.0)
        gap = s - 1.0
        log = LOG_SCALE * jnp.log2(s)
        ratio = gap * pl.reciprocal(s, approx=True)
        one = gap * (log + ratio)
        two = ((ratio - 4.0) * ratio - log) * both[:, 128:]
        one_h, one_l = halves(one)
        two_h, two_l = halves(two)
        weights = jnp.concatenate([jnp.concatenate([one_h, two_h], 1), jnp.concatenate([one_l, two_l], 1)], 0)
        f = f_ref[g]
        out = jnp.dot(jnp.concatenate([f, f], 1), weights, preferred_element_type=F32)
        place = code >> 20
        mask = jnp.where(place < npairs, masks_ref[pl.ds(place, 1), :], 1.0)
        outs.append((own, out * jnp.concatenate([mask, mask], 1)))
    for own, out in outs:
        acc_ref[own] += out


def finish(data_ref, acc_ref, grad_ref, hess_ref):
    nblocks = acc_ref.shape[0]
    row = iota((8, 128), 0)

    def block(b, _):
        start = jnp.minimum(b * 6, nblocks * 6 - 8)
        d = data_ref[pl.ds(start, 8), :]
        d = jnp.where(b == nblocks - 1, pltpu.roll(d, 6, 0), d)
        acc = acc_ref[b]

        def sums(a):
            first, second = a[0:8], a[8:16]
            total = first + second
            low = jnp.where(row == 0, pltpu.roll(first, 1, 0), jnp.where(row < 3, pltpu.roll(second, 3, 0), 0.0))
            return first[6:7], total + low

        n_one, y_one = sums(acc[:, :128] * -0.01)
        n_two, y_two = sums(acc[:, 128:] * 0.02)
        a = d * n_one - y_one
        c = d * n_two - y_two + pltpu.roll(a, 5, 0)
        for k in range(3):
            grad_ref[k, pl.ds(b, 1), :] = a[k : k + 1]
            hess_ref[k, pl.ds(b, 1), :] = c[k : k + 1]
        return 0

    lax.fori_loop(0, nblocks, block, 0)


def task_kernel(lists, capacity, npairs, first, last, *refs):
    list_ref, count_ref, masks_ref, own_ref, data_ref = refs[:5]
    blocks, refs = refs[5 : 5 + len(lists)], refs[5 + len(lists) :]
    if not first:
        before_ref, refs = refs[0], refs[1:]
    if last:
        grad_ref, hess_ref, acc_ref, k_ref, f_ref = refs
    else:
        acc_ref, k_ref, f_ref = refs
    if first:
        acc_ref[...] = jnp.zeros_like(acc_ref)
    else:
        acc_ref[...] = before_ref[...]
    for k, block_ref in zip(lists, blocks):
        count = count_ref[k]
        groups = (count + GROUP - 1) // GROUP

        def codes(i, k=k):
            return [list_ref[k * capacity + i * GROUP + g] for g in range(GROUP)]

        @pl.when(groups > 0)
        def _(block_ref=block_ref, codes=codes, groups=groups):
            prepare(codes(0), block_ref, masks_ref, npairs, k_ref, f_ref)

            def step(i, _):
                accumulate(codes(i), own_ref, masks_ref, npairs, acc_ref, k_ref, f_ref)
                prepare(codes(jnp.minimum(i + 1, groups - 1)), block_ref, masks_ref, npairs, k_ref, f_ref)
                return 0

            lax.fori_loop(0, groups, step, 0)

    if last:
        finish(data_ref, acc_ref, grad_ref, hess_ref)


def tasks(lists, capacity, npairs, list_, count, masks, own, data, blocks, before, last):
    nblocks = own.shape[0]
    acc = jax.ShapeDtypeStruct((nblocks, 16, 256), F32)
    out = jax.ShapeDtypeStruct((3, nblocks, 128), F32)
    first = before is None
    scratch = [pltpu.VMEM((GROUP, 128, 64), BF16), pltpu.VMEM((GROUP, 16, 128), BF16)]
    if last:
        scratch = [pltpu.VMEM(acc.shape, F32)] + scratch
    args = [list_, count, masks, own, data, *blocks] + ([] if first else [before])
    size = sum(b.size for b in blocks) * 4
    return pl.pallas_call(
        functools.partial(task_kernel, lists, capacity, npairs, first, last),
        out_shape=(out, out) if last else acc,
        in_specs=[SMEM, SMEM] + [VMEM] * (len(args) - 2),
        out_specs=(VMEM, VMEM) if last else VMEM,
        scratch_shapes=scratch,
        compiler_params=params(24),
        cost_estimate=pl.CostEstimate(flops=size * 2000, bytes_accessed=size * 3, transcendentals=0),
        name="tasks",
    )(*args)


class Piece:
    def __init__(self, tags, array):
        self.tags, self.array = list(tags), array

    def cut(self, start, stop):
        rows = self.array.shape[0] // len(self.tags)
        return Piece(self.tags[start:stop], self.array[start * rows : stop * rows])


def join(pieces):
    if len(pieces) == 1:
        return pieces[0]
    return Piece(sum([p.tags for p in pieces], []), jnp.concatenate([p.array for p in pieces], axis=0))


def swap(piece, bit, ndev):
    pairs = [(i, i ^ (1 << bit)) for i in range(ndev)]
    return Piece([t ^ (1 << bit) for t in piece.tags], lax.ppermute(piece.array, AXES, pairs))


def tie(piece, other):
    array, _ = lax.optimization_barrier((piece.array, other))
    return Piece(piece.tags, array)


def on_device(positions, direction, pair_local, pair_peer, pair_remote, pair_mask):
    npairs = pair_local.shape[0]
    nblocks = positions.shape[1]
    ndev = lax.axis_size(AXES)
    me = lax.axis_index(AXES).astype(I32)
    slots = max(2, 2 * npairs // ndev)
    stride = -(-(slots + 1) // 8) * 8
    peer, local, remote = (a.reshape(1, npairs) for a in (pair_peer, pair_local, pair_remote))
    data = weave(positions, direction)
    send, mine = pack(ndev, slots, stride, peer, local, remote, pair_mask, data)
    came = lax.all_to_all(send, AXES, split_axis=0, concat_axis=0, tiled=True)

    bits = ndev.bit_length() - 1
    x, y = bits - 2, bits - 1
    column = Piece([0], data)
    for bit in range(bits - 3, 0, -1):
        column = join([column, swap(column, bit, ndev)])
    column.array, came = lax.optimization_barrier((column.array, came))
    over_x, over_y = swap(column, x, ndev), swap(column, y, ndev)
    half = len(column.tags) // 2

    table = np.zeros((1, ndev), np.int32)
    tail = Piece([], jnp.zeros((8, 128), F32))

    def both(k, pieces):
        near = join(pieces + [tail])
        far = swap(near, 0, ndev)
        for which, p in ((2 * k, near), (2 * k + 1, far)):
            for unit, tag in enumerate(p.tags):
                table[0, tag] = which * 256 + unit
        return near.array, far.array

    shape = [
        [column],
        [Piece([t ^ (1 << x) for t in column.tags], None), Piece([t ^ (1 << y) for t in column.tags], None)],
    ]
    diagonal = [t ^ (1 << x) ^ (1 << y) for t in column.tags]
    shape.append([Piece(diagonal[:half], None), Piece(diagonal[half:], None)])
    for k, pieces in enumerate(shape):
        tags = sum([p.tags for p in pieces], [])
        for unit, tag in enumerate(tags):
            table[0, tag] = 2 * k * 256 + unit
            table[0, tag ^ 1] = (2 * k + 1) * 256 + unit
    nlists = 6
    capacity, (list_, count, masks, own) = plan(
        slots, stride, nlists, me.reshape(1), jnp.asarray(table), mine, came, pair_mask, data
    )
    run = functools.partial(tasks, capacity=capacity, npairs=npairs, list_=list_, count=count, masks=masks, own=own, data=data)

    near, far = both(0, [column])
    acc = run(lists=(0, 1), blocks=(near, far), before=None, last=False)
    over_x, over_y = tie(over_x, acc), tie(over_y, acc)
    corner_x, corner_y = swap(over_y.cut(0, half), x, ndev), swap(over_x.cut(half, 2 * half), y, ndev)
    near, far = both(1, [over_x, over_y])
    acc = run(lists=(2,), blocks=(near,), before=acc, last=False)
    acc = run(lists=(3,), blocks=(far,), before=acc, last=False)
    corner_x, corner_y = tie(corner_x, acc), tie(corner_y, acc)
    near, far = both(2, [corner_x, corner_y])
    acc = run(lists=(4,), blocks=(near,), before=acc, last=False)
    return run(lists=(5,), blocks=(far,), before=acc, last=True)


def solution(mesh):
    blocked = P(None, AXES, None)
    in_specs = (blocked, blocked, P(AXES), P(AXES, None), P(AXES), P(AXES, None))
    return jax.shard_map(on_device, mesh=mesh, in_specs=in_specs, out_specs=(blocked, blocked), check_vma=False)
```

```python
import functools

import jax
import jax.numpy as jnp
import numpy as np
from jax import lax
from jax.experimental import pallas as pl
from jax.experimental.pallas import tpu as pltpu
from jax.sharding import PartitionSpec as P

AXES = ("dom", "brick")
F32, BF16, I32 = jnp.float32, jnp.bfloat16, jnp.int32
GROUP = 16
LOG_SCALE = 2.0 * 0.6931471805599453
SMEM = pl.BlockSpec(memory_space=pltpu.SMEM)
VMEM = pl.BlockSpec(memory_space=pltpu.VMEM)
HBM = pl.BlockSpec(memory_space=pltpu.HBM)
ANY = pl.BlockSpec(memory_space=pl.ANY)


def iota(shape, dim):
    return lax.broadcasted_iota(I32, shape, dim)


def params(mib):
    return pltpu.CompilerParams(vmem_limit_bytes=mib << 20)


def fetch(pairs, sems):
    copies = [pltpu.make_async_copy(src, dst, sems.at[i]) for i, (src, dst) in enumerate(pairs)]
    for copy in copies:
        copy.start()
    for copy in copies:
        copy.wait()


def weave_kernel(pos_hbm, dir_hbm, data_ref, pos_ref, dir_ref, sems):
    fetch([(pos_hbm, pos_ref), (dir_hbm, dir_ref)], sems)
    nblocks = pos_ref.shape[1]
    for c in range(3):
        data_ref[pl.ds(c, nblocks, stride=6), :] = pos_ref[c]
        data_ref[pl.ds(3 + c, nblocks, stride=6), :] = dir_ref[c]


def weave(positions, direction):
    nblocks = positions.shape[1]
    whole = pltpu.VMEM(positions.shape, F32)
    return pl.pallas_call(
        weave_kernel,
        out_shape=jax.ShapeDtypeStruct((nblocks * 6, 128), F32),
        in_specs=[HBM] * 2,
        out_specs=VMEM,
        scratch_shapes=[whole, whole, pltpu.SemaphoreType.DMA((2,))],
        compiler_params=params(60),
        name="weave",
    )(positions, direction)


def pack_kernel(
    ndev, slots, stride, peer_hbm, local_hbm, remote_hbm, mask_hbm, data_hbm, send_ref, mine_ref,
    peer_ref, local_ref, remote_ref, mask_ref, sems,
):
    fetch([(peer_hbm, peer_ref), (local_hbm, local_ref), (remote_hbm, remote_ref), (mask_hbm, mask_ref)], sems)
    npairs = peer_ref.shape[1]
    square = (npairs, npairs)
    rows, cols = iota(square, 0), iota(square, 1)

    def column(row):
        return jnp.sum(jnp.where(rows == cols, row, 0), axis=1, keepdims=True)

    peer = peer_ref[...]
    peer_col = column(peer)
    same = peer_col == peer
    rank = jnp.sum(jnp.where(same & (rows < cols), 1, 0), axis=0, keepdims=True)
    rank_col = jnp.sum(jnp.where(same & (cols < rows), 1, 0), axis=1, keepdims=True)
    local_col, remote_col = column(local_ref[...]), column(remote_ref[...])
    lane = iota((npairs, 128), 1)
    part, place = lane // slots, lane % slots
    pair = iota((npairs, 128), 0)
    value = jnp.where(part == 0, local_col, jnp.where(part == 1, remote_col, jnp.where(part == 2, pair, jnp.where(part == 3, 1, 0))))
    numbers = jnp.where(place == rank_col, value, 0).astype(F32).astype(BF16)
    mask = mask_ref[...].astype(F32).astype(BF16)
    slot = iota((ndev * stride, npairs), 0)
    hot = jnp.where(slot == peer * stride + rank, 1.0, 0.0).astype(BF16)
    hot_numbers = jnp.where(slot == peer * stride + slots, 1.0, 0.0).astype(BF16)
    send_ref[...] = jnp.dot(hot, mask, preferred_element_type=F32) + jnp.dot(hot_numbers, numbers, preferred_element_type=F32)
    hot_peer = jnp.where(iota((ndev, npairs), 0) == peer, 1.0, 0.0).astype(BF16)
    mine_ref[...] = jnp.dot(hot_peer, numbers, preferred_element_type=F32)


def pack(ndev, slots, stride, peer, local, remote, mask, data):
    row = pltpu.VMEM(peer.shape, I32)
    return pl.pallas_call(
        functools.partial(pack_kernel, ndev, slots, stride),
        out_shape=(jax.ShapeDtypeStruct((ndev * stride, 128), F32), jax.ShapeDtypeStruct((ndev, 128), F32)),
        in_specs=[HBM] * 4 + [ANY],
        out_specs=(VMEM,) * 2,
        scratch_shapes=[row, row, row, pltpu.VMEM(mask.shape, I32), pltpu.SemaphoreType.DMA((4,))],
        compiler_params=params(60),
        name="pack",
    )(peer, local, remote, mask, data)


def load_block(ref, block):
    last = ref.shape[0] - 8
    start = block * 6
    d = ref[pl.ds(jnp.minimum(start, last), 8), :]
    return jnp.where(start > last, pltpu.roll(d, 6, 0), d)


def split(v):
    h = v.astype(BF16).astype(F32)
    e = v - h
    m = e.astype(BF16).astype(F32)
    return h, m, e - m


def products(d, h, m, row):
    both = h + m
    return both * jnp.where(row < 3, both, pltpu.roll(both, 3, 0))


def other_features(d, row):
    h, m, l = split(d)
    vh, vm, vl = split(products(d, h, m, row))
    hm = jnp.concatenate([h, m], 0).astype(BF16)
    vhm = jnp.concatenate([vh, vm], 0).astype(BF16)
    vlo = jnp.concatenate([vl, jnp.ones_like(d)], 0).astype(BF16)
    first = jnp.where(row < 6, h, jnp.where(row == 6, 1.0, pltpu.roll(l, 7, 0)))
    second = jnp.where(row < 6, m, pltpu.roll(l, 5, 0))
    return jnp.concatenate([hm, hm, vhm, vlo], 0), jnp.concatenate([first, second], 0)


def own_features(d, row):
    d = jnp.where(row < 6, d, 0.0)
    h, m, _ = split(d)
    v = products(d, h, m, row)
    total = v + pltpu.roll(v, 7, 0) + pltpu.roll(v, 6, 0)

    def parts(one_row):
        ph, pm, pl_ = split(jnp.broadcast_to(one_row, d.shape))
        return jnp.where(row == 0, ph, jnp.where(row == 1, pm, jnp.where(row == 2, pl_, 0.0)))

    def cross(a):
        return jnp.where(row < 3, -pltpu.roll(a, 5, 0), jnp.where(row < 6, -pltpu.roll(a, 3, 0), 0.0))

    hs, ms = jnp.where(row < 3, -2.0 * h, 0.0), jnp.where(row < 3, -2.0 * m, 0.0)
    hq, mq = cross(h), cross(m)
    low = jnp.where(row < 3, 1.0, 0.0)
    high = jnp.where((row >= 3) & (row < 6), 1.0, 0.0)
    for_s = jnp.concatenate([hs, ms, ms, hs, low, low, low, parts(total[0:1] + 0.1)], 0)
    for_q = jnp.concatenate([hq, mq, mq, hq, high, high, high, parts(total[3:4])], 0)
    return jnp.concatenate([for_s, for_q], 1).astype(BF16)


def feature_kernel(data_ref, own_ref):
    row = iota((8, 128), 0)

    def feature(i, _):
        for u in range(4):
            own_ref[i * 4 + u] = own_features(load_block(data_ref, i * 4 + u), row)
        return 0

    lax.fori_loop(0, own_ref.shape[0] // 4, feature, 0)


def features(data):
    nblocks = data.shape[0] // 6
    return pl.pallas_call(
        feature_kernel,
        out_shape=jax.ShapeDtypeStruct((nblocks, 64, 256), BF16),
        in_specs=[VMEM],
        out_specs=VMEM,
        compiler_params=params(16),
        name="features",
    )(data)


def plan_kernel(
    slots, stride, sizes, me_ref, order_ref, table_ref, mine_ref, came_ref, mask_ref,
    list_ref, where_ref, masks_ref, code_vmem, code_smem, sem,
):
    ndev = mine_ref.shape[0]
    npairs = mask_ref.shape[0]
    me = me_ref[0]
    lane = iota((ndev, 128), 1)
    peer = iota((ndev, 128), 0)
    rel = iota((ndev, ndev), 0) ^ me
    first_block = jnp.sum(jnp.where(iota((ndev, ndev), 1) == rel, table_ref[...], 0), axis=1, keepdims=True)

    def codes(numbers, mine):
        numbers = numbers.astype(I32)
        second = pltpu.roll(numbers, 128 - slots, 1)
        third = pltpu.roll(numbers, 128 - 2 * slots, 1)
        used = jnp.where((lane >= 3 * slots) & (lane < 4 * slots), numbers, 0)
        count = jnp.sum(used, axis=1, keepdims=True)
        if mine:
            own, other, mask = numbers, second, third
        else:
            own, other, mask = second, numbers, npairs + peer * stride + lane
        code = (first_block + other) + own * (1 << 14) + mask * (1 << 20)
        return jnp.where(lane < slots, code, count)

    code_vmem[0:ndev, :] = codes(mine_ref[...], True)
    code_vmem[ndev:, :] = codes(came_ref[pl.ds(slots, ndev, stride=stride), :], False)
    copy = pltpu.make_async_copy(code_vmem, code_smem, sem)
    copy.start()
    masks_ref[0:npairs, :] = mask_ref[...].astype(F32)
    masks_ref[npairs : npairs + ndev * stride, :] = came_ref[...]
    masks_ref[npairs + ndev * stride :, :] = jnp.zeros((8, 128), F32)
    copy.wait()
    start, done = jnp.int32(0), 0
    for k, size in enumerate(sizes):

        def fill(i, at):
            p = order_ref[i] ^ me
            for row in (p, ndev + p):
                for r in range(slots):
                    list_ref[at + r] = code_smem[row, r]
                at = at + code_smem[row, slots]
            return at

        end = lax.fori_loop(done, done + size, fill, start)
        done += size
        for r in range(GROUP):
            list_ref[end + r] = (npairs + ndev * stride) * (1 << 20)
        groups = (end - start + GROUP - 1) // GROUP
        where_ref[2 * k] = start
        where_ref[2 * k + 1] = groups
        start = start + groups * GROUP


def plan(slots, stride, lists, nblocks, me, mine, came, mask):
    ndev, npairs = mine.shape[0], mask.shape[0]
    order = np.array(sum(lists, []), np.int32)
    table = np.zeros((1, ndev), np.int32)
    for tags in lists:
        table[0, tags] = np.arange(len(tags)) * nblocks
    length = npairs + ndev * slots + len(lists) * GROUP + slots + GROUP
    return pl.pallas_call(
        functools.partial(plan_kernel, slots, stride, [len(tags) for tags in lists]),
        out_shape=(
            jax.ShapeDtypeStruct((length,), I32),
            jax.ShapeDtypeStruct((2 * len(lists),), I32),
            jax.ShapeDtypeStruct((npairs + ndev * stride + 8, 128), F32),
        ),
        in_specs=[SMEM] * 2 + [VMEM] * 4,
        out_specs=(SMEM, SMEM, VMEM),
        scratch_shapes=[pltpu.VMEM((2 * ndev, 128), I32), pltpu.SMEM((2 * ndev, 128), I32), pltpu.SemaphoreType.DMA],
        compiler_params=params(16),
        name="plan",
    )(me, jnp.asarray(order), jnp.asarray(table), mine, came, mask)


def halves(c):
    h = c.astype(BF16)
    return h, (c - h.astype(F32)).astype(BF16)


def prepare(codes, block_ref, masks_ref, npairs, k_ref, f_ref):
    row = iota((8, 128), 0)
    for g, code in enumerate(codes):
        d = load_block(block_ref, code & 0x3FFF)
        left, sums = other_features(d, row)
        place = code >> 20
        mask = jnp.where(place < npairs, 1.0, masks_ref[pl.ds(place, 1), :])
        f_ref[g] = (sums * mask).astype(BF16)
        k_ref[g] = left.T


def accumulate(codes, own_ref, masks_ref, npairs, acc_ref, k_ref, f_ref):
    outs = []
    for g, code in enumerate(codes):
        own = (code >> 14) & 63
        both = jnp.dot(k_ref[g], own_ref[own], preferred_element_type=F32)
        s = jnp.minimum(both[:, :128], 1.0)
        gap = s - 1.0
        log = LOG_SCALE * jnp.log2(s)
        ratio = gap * pl.reciprocal(s, approx=True)
        one = gap * (log + ratio)
        two = ((ratio - 4.0) * ratio - log) * both[:, 128:]
        one_h, one_l = halves(one)
        two_h, two_l = halves(two)
        weights = jnp.concatenate([jnp.concatenate([one_h, two_h], 1), jnp.concatenate([one_l, two_l], 1)], 0)
        f = f_ref[g]
        out = jnp.dot(jnp.concatenate([f, f], 1), weights, preferred_element_type=F32)
        place = code >> 20
        mask = jnp.where(place < npairs, masks_ref[pl.ds(place, 1), :], 1.0)
        outs.append((own, out * jnp.concatenate([mask, mask], 1)))
    for own, out in outs:
        acc_ref[own] += out


def finish(data_ref, acc_ref, grad_ref, hess_ref):
    nblocks = acc_ref.shape[0]
    row = iota((8, 128), 0)

    def block(b, _):
        d = load_block(data_ref, b)
        acc = acc_ref[b]

        def sums(a):
            first, second = a[0:8], a[8:16]
            total = first + second
            low = jnp.where(row == 0, pltpu.roll(first, 1, 0), jnp.where(row < 3, pltpu.roll(second, 3, 0), 0.0))
            return first[6:7], total + low

        n_one, y_one = sums(acc[:, :128] * -0.01)
        n_two, y_two = sums(acc[:, 128:] * 0.02)
        a = d * n_one - y_one
        c = d * n_two - y_two + pltpu.roll(a, 5, 0)
        for k in range(3):
            grad_ref[k, pl.ds(b, 1), :] = a[k : k + 1]
            hess_ref[k, pl.ds(b, 1), :] = c[k : k + 1]
        return 0

    lax.fori_loop(0, nblocks, block, 0)


def task_kernel(lists, npairs, first, last, *refs):
    list_ref, where_ref, masks_ref, own_ref, data_ref = refs[:5]
    blocks, refs = refs[5 : 5 + len(lists)], refs[5 + len(lists) :]
    if not first:
        before_ref, refs = refs[0], refs[1:]
    if last:
        grad_ref, hess_ref, acc_ref, k_ref, f_ref = refs
    else:
        acc_ref, k_ref, f_ref = refs
    if first:
        acc_ref[...] = jnp.zeros_like(acc_ref)
    else:
        acc_ref[...] = before_ref[...]
    for k, block_ref in zip(lists, blocks):
        start, groups = where_ref[2 * k], where_ref[2 * k + 1]

        def codes(i, start=start):
            return [list_ref[start + i * GROUP + g] for g in range(GROUP)]

        @pl.when(groups > 0)
        def _(block_ref=block_ref, codes=codes, groups=groups):
            prepare(codes(0), block_ref, masks_ref, npairs, k_ref, f_ref)

            def step(i, _):
                accumulate(codes(i), own_ref, masks_ref, npairs, acc_ref, k_ref, f_ref)
                prepare(codes(jnp.minimum(i + 1, groups - 1)), block_ref, masks_ref, npairs, k_ref, f_ref)
                return 0

            lax.fori_loop(0, groups, step, 0)

    if last:
        finish(data_ref, acc_ref, grad_ref, hess_ref)


def tasks(lists, npairs, list_, where, masks, own, data, blocks, before, last):
    nblocks = own.shape[0]
    acc = jax.ShapeDtypeStruct((nblocks, 16, 256), F32)
    out = jax.ShapeDtypeStruct((3, nblocks, 128), F32)
    first = before is None
    scratch = [pltpu.VMEM((GROUP, 128, 64), BF16), pltpu.VMEM((GROUP, 16, 128), BF16)]
    if last:
        scratch = [pltpu.VMEM(acc.shape, F32)] + scratch
    args = [list_, where, masks, own, data, *blocks] + ([] if first else [before])
    size = sum(b.size for b in blocks) * 4
    return pl.pallas_call(
        functools.partial(task_kernel, lists, npairs, first, last),
        out_shape=(out, out) if last else acc,
        in_specs=[SMEM, SMEM] + [VMEM] * (len(args) - 2),
        out_specs=(VMEM, VMEM) if last else VMEM,
        scratch_shapes=scratch,
        compiler_params=params(24),
        cost_estimate=pl.CostEstimate(flops=size * 2000, bytes_accessed=size * 3, transcendentals=0),
        name="tasks",
    )(*args)


class Piece:
    def __init__(self, tags, array):
        self.tags, self.array = list(tags), array


def join(pieces):
    if len(pieces) == 1:
        return pieces[0]
    return Piece(sum([p.tags for p in pieces], []), jnp.concatenate([p.array for p in pieces], axis=0))


def swap(piece, bit, ndev):
    pairs = [(i, i ^ (1 << bit)) for i in range(ndev)]
    return Piece([t ^ (1 << bit) for t in piece.tags], lax.ppermute(piece.array, AXES, pairs))


def on_device(positions, direction, pair_local, pair_peer, pair_remote, pair_mask):
    npairs = pair_local.shape[0]
    nblocks = positions.shape[1]
    ndev = lax.axis_size(AXES)
    me = lax.axis_index(AXES).astype(I32)
    slots = max(2, 2 * npairs // ndev)
    stride = -(-(slots + 1) // 8) * 8
    peer, local, remote = (a.reshape(1, npairs) for a in (pair_peer, pair_local, pair_remote))
    data = weave(positions, direction)
    send, mine = pack(ndev, slots, stride, peer, local, remote, pair_mask, data)
    came = lax.all_to_all(send, AXES, split_axis=0, concat_axis=0, tiled=True)
    own = features(data)

    bits = ndev.bit_length() - 1
    x, y = bits - 2, bits - 1
    column = Piece([0], data)
    for bit in range(bits - 3, 0, -1):
        column = join([column, swap(column, bit, ndev)])
    column.array, came = lax.optimization_barrier((column.array, came))

    over_x, over_y = [t ^ (1 << x) for t in column.tags], [t ^ (1 << y) for t in column.tags]
    corner = [t ^ (1 << x) for t in over_y]
    lists = []
    for tags in (column.tags, over_x, over_y, corner):
        lists += [list(tags), [tag ^ 1 for tag in tags]]
    list_, where, masks = plan(slots, stride, lists, nblocks, me.reshape(1), mine, came, pair_mask)
    run = functools.partial(tasks, npairs=npairs, list_=list_, where=where, masks=masks, own=own, data=data)

    over_x, over_y = swap(column, x, ndev), swap(column, y, ndev)
    twin = swap(column, 0, ndev)
    acc = run(lists=(0, 1), blocks=(column.array, twin.array), before=None, last=False)
    over_x.array, over_y.array, acc = lax.optimization_barrier((over_x.array, over_y.array, acc))
    corner = swap(over_y, x, ndev)
    twin_x, twin_y = swap(over_x, 0, ndev), swap(over_y, 0, ndev)
    acc = run(lists=(2, 4), blocks=(over_x.array, over_y.array), before=acc, last=False)
    acc = run(lists=(3, 5), blocks=(twin_x.array, twin_y.array), before=acc, last=False)
    corner.array, acc = lax.optimization_barrier((corner.array, acc))
    twin = swap(corner, 0, ndev)
    acc = run(lists=(6,), blocks=(corner.array,), before=acc, last=False)
    return run(lists=(7,), blocks=(twin.array,), before=acc, last=True)


def solution(mesh):
    blocked = P(None, AXES, None)
    in_specs = (blocked, blocked, P(AXES), P(AXES, None), P(AXES), P(AXES, None))
    return jax.shard_map(on_device, mesh=mesh, in_specs=in_specs, out_specs=(blocked, blocked), check_vma=False)
```

```python
import functools

import jax
import jax.numpy as jnp
import numpy as np
from jax import lax
from jax.experimental import pallas as pl
from jax.experimental.pallas import tpu as pltpu
from jax.sharding import PartitionSpec as P

AXES = ("dom", "brick")
F32, BF16, I32 = jnp.float32, jnp.bfloat16, jnp.int32
GROUP = 32
OWN, MASK = 1 << 12, 1 << 19
LOG_SCALE = 2.0 * 0.6931471805599453
SMEM = pl.BlockSpec(memory_space=pltpu.SMEM)
VMEM = pl.BlockSpec(memory_space=pltpu.VMEM)
HBM = pl.BlockSpec(memory_space=pltpu.HBM)
ANY = pl.BlockSpec(memory_space=pl.ANY)


def iota(shape, dim):
    return lax.broadcasted_iota(I32, shape, dim)


def params(mib):
    return pltpu.CompilerParams(vmem_limit_bytes=mib << 20)


def fetch(pairs, sems):
    copies = [pltpu.make_async_copy(src, dst, sems.at[i]) for i, (src, dst) in enumerate(pairs)]
    for copy in copies:
        copy.start()
    for copy in copies:
        copy.wait()


def weave_kernel(pos_hbm, dir_hbm, data_ref, pos_ref, dir_ref, sems):
    fetch([(pos_hbm, pos_ref), (dir_hbm, dir_ref)], sems)
    nblocks = pos_ref.shape[1]
    for c in range(3):
        data_ref[pl.ds(c, nblocks, stride=6), :] = pos_ref[c]
        data_ref[pl.ds(3 + c, nblocks, stride=6), :] = dir_ref[c]


def weave(positions, direction):
    nblocks = positions.shape[1]
    whole = pltpu.VMEM(positions.shape, F32)
    return pl.pallas_call(
        weave_kernel,
        out_shape=jax.ShapeDtypeStruct((nblocks * 6, 128), F32),
        in_specs=[HBM] * 2,
        out_specs=VMEM,
        scratch_shapes=[whole, whole, pltpu.SemaphoreType.DMA((2,))],
        compiler_params=params(60),
        name="weave",
    )(positions, direction)


def pack_kernel(
    ndev, slots, stride, me_ref, peer_hbm, local_hbm, remote_hbm, mask_hbm, data_hbm, send_ref, keep_ref, give_ref,
    peer_ref, local_ref, remote_ref, mask_ref, sems,
):
    fetch([(peer_hbm, peer_ref), (local_hbm, local_ref), (remote_hbm, remote_ref), (mask_hbm, mask_ref)], sems)
    npairs = peer_ref.shape[1]
    square = (npairs, npairs)
    rows, cols = iota(square, 0), iota(square, 1)

    def column(row):
        return jnp.sum(jnp.where(rows == cols, row, 0), axis=1, keepdims=True)

    peer = peer_ref[...]
    peer_col = column(peer)
    same = peer_col == peer
    rank = jnp.sum(jnp.where(same & (rows < cols), 1, 0), axis=0, keepdims=True)
    rank_col = jnp.sum(jnp.where(same & (cols < rows), 1, 0), axis=1, keepdims=True)
    local_col, remote_col = column(local_ref[...]), column(remote_ref[...])
    lane = iota((npairs, 128), 1)
    part, place = lane // slots, lane % slots
    value = jnp.where(part == 0, local_col, jnp.where(part == 1, remote_col, jnp.where(part == 2, 1, 0)))
    numbers = jnp.where(place == rank_col, value, 0).astype(F32).astype(BF16)
    mask = mask_ref[...].astype(F32).astype(BF16)
    slot = iota((ndev * stride, npairs), 0)

    def chunks(at):
        hot = jnp.where(slot == at * stride + rank, 1.0, 0.0).astype(BF16)
        hot_numbers = jnp.where(slot == at * stride + slots, 1.0, 0.0).astype(BF16)
        return jnp.dot(hot, mask, preferred_element_type=F32) + jnp.dot(hot_numbers, numbers, preferred_element_type=F32)

    send_ref[...] = chunks(peer)
    by_core = chunks(peer // 2 + ((peer ^ me_ref[0]) & 1) * (ndev // 2))
    keep_ref[...] = by_core[: ndev * stride // 2]
    give_ref[...] = by_core[ndev * stride // 2 :]


def pack(ndev, slots, stride, me, peer, local, remote, mask, data):
    row = pltpu.VMEM(peer.shape, I32)
    whole, half = (jax.ShapeDtypeStruct((ndev * stride // k, 128), F32) for k in (1, 2))
    return pl.pallas_call(
        functools.partial(pack_kernel, ndev, slots, stride),
        out_shape=(whole, half, half),
        in_specs=[SMEM] + [HBM] * 4 + [ANY],
        out_specs=(VMEM,) * 3,
        scratch_shapes=[row, row, row, pltpu.VMEM(mask.shape, I32), pltpu.SemaphoreType.DMA((4,))],
        compiler_params=params(60),
        name="pack",
    )(me, peer, local, remote, mask, data)


def load_block(ref, block):
    last = ref.shape[0] - 8
    start = block * 6
    d = ref[pl.ds(jnp.minimum(start, last), 8), :]
    return jnp.where(start > last, pltpu.roll(d, 6, 0), d)


def split(v):
    h = v.astype(BF16).astype(F32)
    e = v - h
    m = e.astype(BF16).astype(F32)
    return h, m, e - m


def products(d, h, m, row):
    both = h + m
    return both * jnp.where(row < 3, both, pltpu.roll(both, 3, 0))


def other_features(d, row):
    h, m, l = split(d)
    vh, vm, vl = split(products(d, h, m, row))
    hm = jnp.concatenate([h, m], 0).astype(BF16)
    vhm = jnp.concatenate([vh, vm], 0).astype(BF16)
    vlo = jnp.concatenate([vl, jnp.ones_like(d)], 0).astype(BF16)
    first = jnp.where(row < 6, h, jnp.where(row == 6, 1.0, pltpu.roll(l, 7, 0)))
    second = jnp.where(row < 6, m, pltpu.roll(l, 5, 0))
    return jnp.concatenate([hm, hm, vhm, vlo], 0), jnp.concatenate([first, second], 0)


def own_features(d, row):
    d = jnp.where(row < 6, d, 0.0)
    h, m, _ = split(d)
    v = products(d, h, m, row)
    total = v + pltpu.roll(v, 7, 0) + pltpu.roll(v, 6, 0)

    def parts(one_row):
        ph, pm, pl_ = split(jnp.broadcast_to(one_row, d.shape))
        return jnp.where(row == 0, ph, jnp.where(row == 1, pm, jnp.where(row == 2, pl_, 0.0)))

    def cross(a):
        return jnp.where(row < 3, -pltpu.roll(a, 5, 0), jnp.where(row < 6, -pltpu.roll(a, 3, 0), 0.0))

    hs, ms = jnp.where(row < 3, -2.0 * h, 0.0), jnp.where(row < 3, -2.0 * m, 0.0)
    hq, mq = cross(h), cross(m)
    low = jnp.where(row < 3, 1.0, 0.0)
    high = jnp.where((row >= 3) & (row < 6), 1.0, 0.0)
    for_s = jnp.concatenate([hs, ms, ms, hs, low, low, low, parts(total[0:1] + 0.1)], 0)
    for_q = jnp.concatenate([hq, mq, mq, hq, high, high, high, parts(total[3:4])], 0)
    return jnp.concatenate([for_s, for_q], 1).astype(BF16)


def plan_kernel(
    slots, stride, sizes, me_ref, order_ref, table_ref, keep_ref, got_ref, came_ref, data_ref, sibling_ref,
    list_ref, where_ref, masks_ref, own_ref, code_vmem, code_smem, sem,
):
    chips = keep_ref.shape[0] // stride
    nblocks = own_ref.shape[0] // 2
    me = me_ref[0]
    mine, core = me // 2, me % 2
    lane = iota((chips, 128), 1)
    chip = iota((chips, 128), 0)
    rel = iota((chips, chips), 0) ^ mine
    first_block = jnp.sum(jnp.where(iota((chips, chips), 1) == rel, table_ref[...], 0), axis=1, keepdims=True)

    def dense(rows, first):
        total = jnp.zeros((8, 128), I32)
        for j in range(chips // 8):
            total += pltpu.roll(jnp.where(lane[:8] < slots, rows[8 * j : 8 * j + 8], 0), first + j * slots, 1)
        return total

    code, count = jnp.zeros((8, 128), I32), jnp.zeros((8, 128), I32)
    span = chips // 8 * slots
    sides = (
        (keep_ref[pl.ds(slots, chips, stride=stride), :], True, 0, chip * stride),
        (got_ref[pl.ds(slots, chips, stride=stride), :], True, nblocks, (chips + chip) * stride),
        (came_ref[pl.ds(slots, chips, stride=2 * stride), :], False, core * nblocks, (2 * chips + 2 * chip) * stride),
        (came_ref[pl.ds(slots + stride, chips, stride=2 * stride), :], False, (1 - core) * nblocks, (2 * chips + 2 * chip + 1) * stride),
    )
    for i, (numbers, left, base, mask) in enumerate(sides):
        numbers = numbers.astype(I32)
        second = pltpu.roll(numbers, 128 - slots, 1)
        used = jnp.where((lane >= 2 * slots) & (lane < 3 * slots), numbers, 0)
        own, other = (numbers, second) if left else (second, numbers)
        code += dense((first_block + other) + (own + base) * OWN + (mask + lane) * MASK, i * span)
        count += dense(jnp.broadcast_to(jnp.sum(used, axis=1, keepdims=True), numbers.shape), i * span)
    code_vmem[0] = code
    code_vmem[1] = count
    copy = pltpu.make_async_copy(code_vmem, code_smem, sem)
    copy.start()
    masks_ref[: chips * stride, :] = keep_ref[...]
    masks_ref[chips * stride :, :] = got_ref[...]
    row = iota((8, 128), 0)

    def feature(i, _):
        for u in range(2):
            own_ref[i * 2 + u] = own_features(load_block(data_ref, i * 2 + u), row)
            own_ref[nblocks + i * 2 + u] = own_features(load_block(sibling_ref, i * 2 + u), row)
        return 0

    lax.fori_loop(0, nblocks // 2, feature, 0)
    copy.wait()
    start, done = jnp.int32(0), 0
    for k, size in enumerate(sizes):

        def fill(i, at):
            p = order_ref[i] ^ mine
            line, lanes = p % 8, p // 8 * slots
            for side in range(len(sides)):
                for r in range(slots):
                    list_ref[at + r] = code_smem[0, line, lanes + side * span + r]
                at = at + code_smem[1, line, lanes + side * span]
            return at

        end = lax.fori_loop(done, done + size, fill, start)
        done += size
        for r in range(GROUP):
            list_ref[end + r] = (2 * chips * stride + slots + 1) * MASK
        groups = (end - start + GROUP - 1) // GROUP
        where_ref[2 * k] = start
        where_ref[2 * k + 1] = groups
        start = start + groups * GROUP


def plan(slots, stride, lists, me, keep, got, came, data, sibling):
    chips, nblocks = keep.shape[0] // stride, data.shape[0] // 6
    order = np.array(sum(lists, []), np.int32) // 2
    table = np.zeros((1, chips), np.int32)
    for tags in lists:
        table[0, np.array(tags) // 2] = np.arange(len(tags)) * nblocks
    length = 4 * chips * slots + len(lists) * GROUP + slots + GROUP
    return pl.pallas_call(
        functools.partial(plan_kernel, slots, stride, [len(tags) for tags in lists]),
        out_shape=(
            jax.ShapeDtypeStruct((length,), I32),
            jax.ShapeDtypeStruct((2 * len(lists),), I32),
            jax.ShapeDtypeStruct((2 * chips * stride, 128), F32),
            jax.ShapeDtypeStruct((2 * nblocks, 64, 256), BF16),
        ),
        in_specs=[SMEM] * 2 + [VMEM] * 6,
        out_specs=(SMEM, SMEM, VMEM, VMEM),
        scratch_shapes=[pltpu.VMEM((2, 8, 128), I32), pltpu.SMEM((2, 8, 128), I32), pltpu.SemaphoreType.DMA],
        compiler_params=params(24),
        name="plan",
    )(me, jnp.asarray(order), jnp.asarray(table), keep, got, came, data, sibling)


def halves(c):
    h = c.astype(BF16)
    return h, (c - h.astype(F32)).astype(BF16)


def prepare(codes, block_ref, came_ref, nleft, k_ref, f_ref):
    row = iota((8, 128), 0)
    for g, code in enumerate(codes):
        d = load_block(block_ref, code % OWN)
        left, sums = other_features(d, row)
        place = code // MASK - nleft
        mask = jnp.where(place < 0, 1.0, came_ref[pl.ds(jnp.maximum(place, 0), 1), :])
        f_ref[g] = (sums * mask).astype(BF16)
        k_ref[g] = left.T


def accumulate(codes, own_ref, mask_ref, acc_ref, k_ref, f_ref):
    nleft = mask_ref.shape[0]
    outs = []
    for g, code in enumerate(codes):
        own = code // OWN % (MASK // OWN)
        both = jnp.dot(k_ref[g], own_ref[own], preferred_element_type=F32)
        s = jnp.minimum(both[:, :128], 1.0)
        gap = s - 1.0
        log = LOG_SCALE * jnp.log2(s)
        ratio = gap * pl.reciprocal(s, approx=True)
        one = gap * (log + ratio)
        two = ((ratio - 4.0) * ratio - log) * both[:, 128:]
        one_h, one_l = halves(one)
        two_h, two_l = halves(two)
        weights = jnp.concatenate([jnp.concatenate([one_h, two_h], 1), jnp.concatenate([one_l, two_l], 1)], 0)
        f = f_ref[g]
        out = jnp.dot(jnp.concatenate([f, f], 1), weights, preferred_element_type=F32)
        place = code // MASK
        mask = mask_ref[pl.ds(jnp.minimum(place, nleft - 1), 1), :]
        mask = jnp.where(place < nleft, mask, 1.0)
        outs.append((own, out * jnp.concatenate([mask, mask], 1)))
    for own, out in outs:
        acc_ref[own] += out


def finish(data_ref, first, acc_ref, out_ref):
    nblocks = out_ref.shape[2]
    row = iota((8, 128), 0)

    def block(b):
        d = load_block(data_ref, b)
        acc = acc_ref[first + b]

        def sums(a):
            first, second = a[0:8], a[8:16]
            total = first + second
            low = jnp.where(row == 0, pltpu.roll(first, 1, 0), jnp.where(row < 3, pltpu.roll(second, 3, 0), 0.0))
            return first[6:7], total + low

        n_one, y_one = sums(acc[:, :128] * -0.01)
        n_two, y_two = sums(acc[:, 128:] * 0.02)
        a = d * n_one - y_one
        c = d * n_two - y_two + pltpu.roll(a, 5, 0)
        for k in range(3):
            out_ref[0, k, pl.ds(b, 1), :] = a[k : k + 1]
            out_ref[1, k, pl.ds(b, 1), :] = c[k : k + 1]

    def some(i, _):
        for u in range(4):
            block(i * 4 + u)
        return 0

    lax.fori_loop(0, nblocks // 4, some, 0)


def task_kernel(which, count, first, last, *refs):
    list_ref, where_ref, mask_ref, came_ref, own_ref, data_ref, sibling_ref = refs[:7]
    nleft = mask_ref.shape[0]
    arrays, refs = refs[7 : 7 + count], refs[7 + count :]
    if not first:
        before_ref, refs = refs[0], refs[1:]
    if last:
        mine_ref, other_ref, acc_ref, k_ref, f_ref = refs[:5]
    else:
        acc_ref, k_ref, f_ref = refs[:3]
    if count == 1:
        block_ref = arrays[0]
    else:
        block_ref, sems = refs[-2:]
        rows = arrays[0].shape[0]
        copies = [
            pltpu.make_async_copy(array, block_ref.at[pl.ds(i * rows, rows), :], sems.at[i]) for i, array in enumerate(arrays)
        ]
        for copy in copies:
            copy.start()
    if first:
        acc_ref[...] = jnp.zeros_like(acc_ref)
    else:
        acc_ref[...] = before_ref[...]
    if count > 1:
        for copy in copies:
            copy.wait()
    start, groups = where_ref[2 * which], where_ref[2 * which + 1]

    def codes(i):
        return [list_ref[start + i * GROUP + g] for g in range(GROUP)]

    @pl.when(groups > 0)
    def _():
        prepare(codes(0), block_ref, came_ref, nleft, k_ref, f_ref)

        def step(i, _):
            accumulate(codes(i), own_ref, mask_ref, acc_ref, k_ref, f_ref)
            prepare(codes(jnp.minimum(i + 1, groups - 1)), block_ref, came_ref, nleft, k_ref, f_ref)
            return 0

        lax.fori_loop(0, groups, step, 0)

    if last:
        nblocks = mine_ref.shape[2]
        finish(sibling_ref, nblocks, acc_ref, other_ref)
        finish(data_ref, 0, acc_ref, mine_ref)


def tasks(which, list_, where, mask, came, own, data, sibling, blocks, before, last):
    nblocks = own.shape[0] // 2
    acc = jax.ShapeDtypeStruct((2 * nblocks, 16, 256), F32)
    out = jax.ShapeDtypeStruct((2, 3, nblocks, 128), F32)
    first = before is None
    count = len(blocks)
    scratch = [pltpu.VMEM((GROUP, 128, 64), BF16), pltpu.VMEM((GROUP, 16, 128), BF16)]
    if last:
        scratch = [pltpu.VMEM(acc.shape, F32)] + scratch
    if count > 1:
        scratch += [pltpu.VMEM((count * blocks[0].shape[0], 128), F32), pltpu.SemaphoreType.DMA((count,))]
    args = [list_, where, mask, came, own, data, sibling, *blocks] + ([] if first else [before])
    size = sum(b.size for b in blocks) * 4
    return pl.pallas_call(
        functools.partial(task_kernel, which, count, first, last),
        out_shape=(out, out) if last else acc,
        in_specs=[SMEM, SMEM] + [VMEM] * 5 + [VMEM if count == 1 else ANY] * count + ([] if first else [VMEM]),
        out_specs=(VMEM, VMEM) if last else VMEM,
        scratch_shapes=scratch,
        compiler_params=params(32),
        cost_estimate=pl.CostEstimate(flops=size * 2000, bytes_accessed=size * 3, transcendentals=0),
        name="tasks",
    )(*args)


class Piece:
    def __init__(self, tags, array):
        self.tags, self.array = list(tags), array


def join(pieces):
    if len(pieces) == 1:
        return pieces[0]
    return Piece(sum([p.tags for p in pieces], []), jnp.concatenate([p.array for p in pieces], axis=0))


def swap(piece, bit, ndev):
    pairs = [(i, i ^ (1 << bit)) for i in range(ndev)]
    return Piece([t ^ (1 << bit) for t in piece.tags], lax.ppermute(piece.array, AXES, pairs))


def on_device(positions, direction, pair_local, pair_peer, pair_remote, pair_mask):
    npairs = pair_local.shape[0]
    ndev = lax.axis_size(AXES)
    me = lax.axis_index(AXES).astype(I32).reshape(1)
    slots = max(2, 2 * npairs // ndev)
    stride = -(-(slots + 2) // 8) * 8
    peer, local, remote = (a.reshape(1, npairs) for a in (pair_peer, pair_local, pair_remote))
    data = weave(positions, direction)
    send, keep, give = pack(ndev, slots, stride, me, peer, local, remote, pair_mask, data)
    groups = [list(range(core, ndev, 2)) for core in range(2)]
    came = lax.all_to_all(send, AXES, split_axis=0, concat_axis=0, axis_index_groups=groups, tiled=True)
    siblings = [(i, i ^ 1) for i in range(ndev)]
    sibling = lax.ppermute(data, AXES, siblings)
    got = lax.ppermute(give, AXES, siblings)

    bits = ndev.bit_length() - 1
    x, y = bits - 2, bits - 1
    column = Piece([0], data)
    for bit in range(bits - 3, 0, -1):
        column = join([column, swap(column, bit, ndev)])
    column.array, came = lax.optimization_barrier((column.array, came))

    over_x, over_y = [t ^ (1 << x) for t in column.tags], [t ^ (1 << y) for t in column.tags]
    corner = [t ^ (1 << x) for t in over_y]
    list_, where, masks, own = plan(slots, stride, [column.tags, over_x + over_y, corner], me, keep, got, came, data, sibling)
    run = functools.partial(tasks, list_=list_, where=where, mask=masks, came=came, own=own, data=data, sibling=sibling)

    over_x, over_y = swap(column, x, ndev), swap(column, y, ndev)
    acc = run(0, blocks=(column.array,), before=None, last=False)
    over_x.array, over_y.array, acc = lax.optimization_barrier((over_x.array, over_y.array, acc))
    corner = swap(over_y, x, ndev)
    acc = run(1, blocks=(over_x.array, over_y.array), before=acc, last=False)
    corner.array, acc = lax.optimization_barrier((corner.array, acc))
    mine, other = run(2, blocks=(corner.array,), before=acc, last=True)
    total = mine + lax.ppermute(other, AXES, siblings)
    return total[0], total[1]


def solution(mesh):
    blocked = P(None, AXES, None)
    in_specs = (blocked, blocked, P(AXES), P(AXES, None), P(AXES), P(AXES, None))
    return jax.shard_map(on_device, mesh=mesh, in_specs=in_specs, out_specs=(blocked, blocked), check_vma=False)
```

```python
import functools

import jax
import jax.numpy as jnp
import numpy as np
from jax import lax
from jax.experimental import pallas as pl
from jax.experimental.pallas import tpu as pltpu
from jax.sharding import PartitionSpec as P

AXES = ("dom", "brick")
F32, BF16, I32 = jnp.float32, jnp.bfloat16, jnp.int32
GROUP = 32
OWN, MASK = 1 << 12, 1 << 19
LOG_SCALE = 2.0 * 0.6931471805599453
SMEM = pl.BlockSpec(memory_space=pltpu.SMEM)
VMEM = pl.BlockSpec(memory_space=pltpu.VMEM)
HBM = pl.BlockSpec(memory_space=pltpu.HBM)
ANY = pl.BlockSpec(memory_space=pl.ANY)


def iota(shape, dim):
    return lax.broadcasted_iota(I32, shape, dim)


def params(mib):
    return pltpu.CompilerParams(vmem_limit_bytes=mib << 20)


def fetch(pairs, sems):
    copies = [pltpu.make_async_copy(src, dst, sems.at[i]) for i, (src, dst) in enumerate(pairs)]
    for copy in copies:
        copy.start()
    for copy in copies:
        copy.wait()


def weave_kernel(pos_hbm, dir_hbm, data_ref, pos_ref, dir_ref, sems):
    fetch([(pos_hbm, pos_ref), (dir_hbm, dir_ref)], sems)
    nblocks = pos_ref.shape[1]
    for c in range(3):
        data_ref[pl.ds(c, nblocks, stride=6), :] = pos_ref[c]
        data_ref[pl.ds(3 + c, nblocks, stride=6), :] = dir_ref[c]


def weave(positions, direction):
    nblocks = positions.shape[1]
    whole = pltpu.VMEM(positions.shape, F32)
    return pl.pallas_call(
        weave_kernel,
        out_shape=jax.ShapeDtypeStruct((nblocks * 6, 128), F32),
        in_specs=[HBM] * 2,
        out_specs=VMEM,
        scratch_shapes=[whole, whole, pltpu.SemaphoreType.DMA((2,))],
        compiler_params=params(60),
        name="weave",
    )(positions, direction)


def pack_kernel(
    ndev, slots, stride, me_ref, peer_hbm, local_hbm, remote_hbm, mask_hbm, data_hbm, send_ref, keep_ref, give_ref,
    peer_ref, local_ref, remote_ref, mask_ref, sems,
):
    fetch([(peer_hbm, peer_ref), (local_hbm, local_ref), (remote_hbm, remote_ref), (mask_hbm, mask_ref)], sems)
    npairs = peer_ref.shape[1]
    square = (npairs, npairs)
    rows, cols = iota(square, 0), iota(square, 1)

    def column(row):
        return jnp.sum(jnp.where(rows == cols, row, 0), axis=1, keepdims=True)

    peer = peer_ref[...]
    peer_col = column(peer)
    same = peer_col == peer
    rank = jnp.sum(jnp.where(same & (rows < cols), 1, 0), axis=0, keepdims=True)
    rank_col = jnp.sum(jnp.where(same & (cols < rows), 1, 0), axis=1, keepdims=True)
    local_col, remote_col = column(local_ref[...]), column(remote_ref[...])
    lane = iota((npairs, 128), 1)
    part, place = lane // slots, lane % slots
    value = jnp.where(part == 0, local_col, jnp.where(part == 1, remote_col, jnp.where(part == 2, 1, 0)))
    numbers = jnp.where(place == rank_col, value, 0).astype(F32).astype(BF16)
    mask = mask_ref[...].astype(F32).astype(BF16)
    slot = iota((ndev * stride, npairs), 0)

    def chunks(at):
        hot = jnp.where(slot == at * stride + rank, 1.0, 0.0).astype(BF16)
        hot_numbers = jnp.where(slot == at * stride + slots, 1.0, 0.0).astype(BF16)
        return jnp.dot(hot, mask, preferred_element_type=F32) + jnp.dot(hot_numbers, numbers, preferred_element_type=F32)

    send_ref[...] = chunks(peer)
    by_core = chunks(peer // 2 + ((peer ^ me_ref[0]) & 1) * (ndev // 2))
    keep_ref[...] = by_core[: ndev * stride // 2]
    give_ref[...] = by_core[ndev * stride // 2 :]


def pack(ndev, slots, stride, me, peer, local, remote, mask, data):
    row = pltpu.VMEM(peer.shape, I32)
    whole, half = (jax.ShapeDtypeStruct((ndev * stride // k, 128), F32) for k in (1, 2))
    return pl.pallas_call(
        functools.partial(pack_kernel, ndev, slots, stride),
        out_shape=(whole, half, half),
        in_specs=[SMEM] + [HBM] * 4 + [ANY],
        out_specs=(VMEM,) * 3,
        scratch_shapes=[row, row, row, pltpu.VMEM(mask.shape, I32), pltpu.SemaphoreType.DMA((4,))],
        compiler_params=params(60),
        name="pack",
    )(me, peer, local, remote, mask, data)


def load_block(ref, block):
    last = ref.shape[0] - 8
    start = block * 6
    d = ref[pl.ds(jnp.minimum(start, last), 8), :]
    return jnp.where(start > last, pltpu.roll(d, 6, 0), d)


def split(v):
    h = v.astype(BF16).astype(F32)
    e = v - h
    m = e.astype(BF16).astype(F32)
    return h, m, e - m


def products(d, h, m, row):
    both = h + m
    return both * jnp.where(row < 3, both, pltpu.roll(both, 3, 0))


def other_features(d, row):
    h, m, l = split(d)
    vh, vm, vl = split(products(d, h, m, row))
    hm = jnp.concatenate([h, m], 0).astype(BF16)
    vhm = jnp.concatenate([vh, vm], 0).astype(BF16)
    vlo = jnp.concatenate([vl, jnp.ones_like(d)], 0).astype(BF16)
    first = jnp.where(row < 6, h, jnp.where(row == 6, 1.0, pltpu.roll(l, 7, 0)))
    second = jnp.where(row < 6, m, pltpu.roll(l, 5, 0))
    return jnp.concatenate([hm, hm, vhm, vlo], 0), jnp.concatenate([first, second], 0)


def own_features(d, row):
    d = jnp.where(row < 6, d, 0.0)
    h, m, _ = split(d)
    v = products(d, h, m, row)
    total = v + pltpu.roll(v, 7, 0) + pltpu.roll(v, 6, 0)

    def parts(one_row):
        ph, pm, pl_ = split(jnp.broadcast_to(one_row, d.shape))
        return jnp.where(row == 0, ph, jnp.where(row == 1, pm, jnp.where(row == 2, pl_, 0.0)))

    def cross(a):
        return jnp.where(row < 3, -pltpu.roll(a, 5, 0), jnp.where(row < 6, -pltpu.roll(a, 3, 0), 0.0))

    hs, ms = jnp.where(row < 3, -2.0 * h, 0.0), jnp.where(row < 3, -2.0 * m, 0.0)
    hq, mq = cross(h), cross(m)
    low = jnp.where(row < 3, 1.0, 0.0)
    high = jnp.where((row >= 3) & (row < 6), 1.0, 0.0)
    for_s = jnp.concatenate([hs, ms, ms, hs, low, low, low, parts(total[0:1] + 0.1)], 0)
    for_q = jnp.concatenate([hq, mq, mq, hq, high, high, high, parts(total[3:4])], 0)
    return jnp.concatenate([for_s, for_q], 1).astype(BF16)


def plan_kernel(
    slots, stride, sizes, me_ref, order_ref, table_ref, keep_ref, got_ref, came_ref, data_ref, sibling_ref,
    list_ref, where_ref, masks_ref, own_ref, code_vmem, code_smem, sem,
):
    chips = keep_ref.shape[0] // stride
    nblocks = own_ref.shape[0] // 2
    me = me_ref[0]
    mine, core = me // 2, me % 2
    lane = iota((chips, 128), 1)
    chip = iota((chips, 128), 0)
    rel = iota((chips, chips), 0) ^ mine
    first_block = jnp.sum(jnp.where(iota((chips, chips), 1) == rel, table_ref[...], 0), axis=1, keepdims=True)

    code = jnp.zeros((chips, 128), I32)
    sides = (
        (keep_ref[pl.ds(slots, chips, stride=stride), :], True, 0, chip * stride),
        (got_ref[pl.ds(slots, chips, stride=stride), :], True, nblocks, (chips + chip) * stride),
        (came_ref[pl.ds(slots, chips, stride=2 * stride), :], False, core * nblocks, (2 * chips + 2 * chip) * stride),
        (came_ref[pl.ds(slots + stride, chips, stride=2 * stride), :], False, (1 - core) * nblocks, (2 * chips + 2 * chip + 1) * stride),
    )
    for i, (numbers, left, base, mask) in enumerate(sides):
        numbers = numbers.astype(I32)
        second = pltpu.roll(numbers, 128 - slots, 1)
        used = jnp.where((lane >= 2 * slots) & (lane < 3 * slots), numbers, 0)
        own, other = (numbers, second) if left else (second, numbers)
        part = jnp.where(lane < slots, (first_block + other) + (own + base) * OWN + (mask + lane) * MASK, 0)
        code += pltpu.roll(part, i * slots, 1) if i else part
        code += jnp.where(lane == len(sides) * slots + i, jnp.sum(used, axis=1, keepdims=True), 0)
    code_vmem[...] = code
    copy = pltpu.make_async_copy(code_vmem, code_smem, sem)
    copy.start()
    masks_ref[: chips * stride, :] = keep_ref[...]
    masks_ref[chips * stride :, :] = got_ref[...]
    row = iota((8, 128), 0)

    def feature(i, _):
        for u in range(4):
            own_ref[i * 4 + u] = own_features(load_block(data_ref, i * 4 + u), row)
            own_ref[nblocks + i * 4 + u] = own_features(load_block(sibling_ref, i * 4 + u), row)
        return 0

    lax.fori_loop(0, nblocks // 4, feature, 0)
    copy.wait()
    start, done = jnp.int32(0), 0
    for k, size in enumerate(sizes):

        def fill(i, at):
            p = order_ref[i] ^ mine
            counts = [code_smem[p, len(sides) * slots + side] for side in range(len(sides))]
            for side, count in enumerate(counts):
                held = [code_smem[p, side * slots + r] for r in range(slots)]
                for r in range(slots):
                    list_ref[at + r] = held[r]
                at = at + count
            return at

        end = lax.fori_loop(done, done + size, fill, start)
        done += size
        for r in range(GROUP):
            list_ref[end + r] = (2 * chips * stride + slots + 1) * MASK
        groups = (end - start + GROUP - 1) // GROUP
        where_ref[2 * k] = start
        where_ref[2 * k + 1] = groups
        start = start + groups * GROUP


def plan(slots, stride, lists, me, keep, got, came, data, sibling):
    chips, nblocks = keep.shape[0] // stride, data.shape[0] // 6
    order = np.array(sum(lists, []), np.int32) // 2
    table = np.zeros((1, chips), np.int32)
    for tags in lists:
        table[0, np.array(tags) // 2] = np.arange(len(tags)) * nblocks
    length = 4 * chips * slots + len(lists) * GROUP + slots + GROUP
    return pl.pallas_call(
        functools.partial(plan_kernel, slots, stride, [len(tags) for tags in lists]),
        out_shape=(
            jax.ShapeDtypeStruct((length,), I32),
            jax.ShapeDtypeStruct((2 * len(lists),), I32),
            jax.ShapeDtypeStruct((2 * chips * stride, 128), F32),
            jax.ShapeDtypeStruct((2 * nblocks, 64, 256), BF16),
        ),
        in_specs=[SMEM] * 2 + [VMEM] * 6,
        out_specs=(SMEM, SMEM, VMEM, VMEM),
        scratch_shapes=[pltpu.VMEM((chips, 128), I32), pltpu.SMEM((chips, 128), I32), pltpu.SemaphoreType.DMA],
        compiler_params=params(24),
        name="plan",
    )(me, jnp.asarray(order), jnp.asarray(table), keep, got, came, data, sibling)


def halves(c):
    h = c.astype(BF16)
    return h, (c - h.astype(F32)).astype(BF16)


def prepare(codes, block_ref, came_ref, nleft, k_ref, f_ref):
    row = iota((8, 128), 0)
    for g, code in enumerate(codes):
        d = load_block(block_ref, code % OWN)
        left, sums = other_features(d, row)
        place = code // MASK - nleft
        mask = jnp.where(place < 0, 1.0, came_ref[pl.ds(jnp.maximum(place, 0), 1), :])
        f_ref[g] = (sums * mask).astype(BF16)
        k_ref[g] = left.T


def accumulate(codes, own_ref, mask_ref, acc_ref, k_ref, f_ref):
    nleft = mask_ref.shape[0]
    outs = []
    for g, code in enumerate(codes):
        own = code // OWN % (MASK // OWN)
        both = jnp.dot(k_ref[g], own_ref[own], preferred_element_type=F32)
        s = jnp.minimum(both[:, :128], 1.0)
        gap = s - 1.0
        log = LOG_SCALE * jnp.log2(s)
        ratio = gap * pl.reciprocal(s, approx=True)
        one = gap * (log + ratio)
        two = ((ratio - 4.0) * ratio - log) * both[:, 128:]
        one_h, one_l = halves(one)
        two_h, two_l = halves(two)
        weights = jnp.concatenate([jnp.concatenate([one_h, two_h], 1), jnp.concatenate([one_l, two_l], 1)], 0)
        f = f_ref[g]
        out = jnp.dot(jnp.concatenate([f, f], 1), weights, preferred_element_type=F32)
        place = code // MASK
        mask = mask_ref[pl.ds(jnp.minimum(place, nleft - 1), 1), :]
        mask = jnp.where(place < nleft, mask, 1.0)
        outs.append((own, out * jnp.concatenate([mask, mask], 1)))
    for own, out in outs:
        acc_ref[own] += out


def finish(data_ref, first, acc_ref, out_ref):
    nblocks = out_ref.shape[2]
    row = iota((8, 128), 0)

    def block(b):
        d = load_block(data_ref, b)
        acc = acc_ref[first + b]

        def sums(a):
            first, second = a[0:8], a[8:16]
            total = first + second
            low = jnp.where(row == 0, pltpu.roll(first, 1, 0), jnp.where(row < 3, pltpu.roll(second, 3, 0), 0.0))
            return first[6:7], total + low

        n_one, y_one = sums(acc[:, :128] * -0.01)
        n_two, y_two = sums(acc[:, 128:] * 0.02)
        a = d * n_one - y_one
        c = d * n_two - y_two + pltpu.roll(a, 5, 0)
        for k in range(3):
            out_ref[0, k, pl.ds(b, 1), :] = a[k : k + 1]
            out_ref[1, k, pl.ds(b, 1), :] = c[k : k + 1]

    def some(i, _):
        for u in range(16):
            block(i * 16 + u)
        return 0

    lax.fori_loop(0, nblocks // 16, some, 0)


def task_kernel(which, count, first, last, *refs):
    list_ref, where_ref, mask_ref, came_ref, own_ref, sibling_ref = refs[:6]
    nleft = mask_ref.shape[0]
    arrays, refs = refs[6 : 6 + count], refs[6 + count :]
    if not first:
        before_ref, refs = refs[0], refs[1:]
    if last:
        other_ref, refs = refs[0], refs[1:]
    acc_ref, k_ref, f_ref = refs[:3]
    if count == 1:
        block_ref = arrays[0]
    else:
        block_ref, sems = refs[-2:]
        rows = arrays[0].shape[0]
        copies = [
            pltpu.make_async_copy(array, block_ref.at[pl.ds(i * rows, rows), :], sems.at[i]) for i, array in enumerate(arrays)
        ]
        for copy in copies:
            copy.start()
    if first:
        acc_ref[...] = jnp.zeros_like(acc_ref)
    else:
        acc_ref[...] = before_ref[...]
    if count > 1:
        for copy in copies:
            copy.wait()
    start, groups = where_ref[2 * which], where_ref[2 * which + 1]

    def codes(i):
        return [list_ref[start + i * GROUP + g] for g in range(GROUP)]

    @pl.when(groups > 0)
    def _():
        prepare(codes(0), block_ref, came_ref, nleft, k_ref, f_ref)

        def step(i, _):
            accumulate(codes(i), own_ref, mask_ref, acc_ref, k_ref, f_ref)
            prepare(codes(jnp.minimum(i + 1, groups - 1)), block_ref, came_ref, nleft, k_ref, f_ref)
            return 0

        lax.fori_loop(0, groups, step, 0)

    if last:
        finish(sibling_ref, other_ref.shape[2], acc_ref, other_ref)


def tasks(which, list_, where, mask, came, own, sibling, blocks, before, last):
    nblocks = own.shape[0] // 2
    acc = jax.ShapeDtypeStruct((2 * nblocks, 16, 256), F32)
    out = jax.ShapeDtypeStruct((2, 3, nblocks, 128), F32)
    first = before is None
    count = len(blocks)
    scratch = [pltpu.VMEM((GROUP, 128, 64), BF16), pltpu.VMEM((GROUP, 16, 128), BF16)]
    if count > 1:
        scratch += [pltpu.VMEM((count * blocks[0].shape[0], 128), F32), pltpu.SemaphoreType.DMA((count,))]
    args = [list_, where, mask, came, own, sibling, *blocks] + ([] if first else [before])
    size = sum(b.size for b in blocks) * 4
    return pl.pallas_call(
        functools.partial(task_kernel, which, count, first, last),
        out_shape=(out, acc) if last else acc,
        in_specs=[SMEM, SMEM] + [VMEM] * 4 + [VMEM if count == 1 else ANY] * count + ([] if first else [VMEM]),
        out_specs=(VMEM, VMEM) if last else VMEM,
        scratch_shapes=scratch,
        compiler_params=params(16),
        cost_estimate=pl.CostEstimate(flops=size * 2000, bytes_accessed=size * 3, transcendentals=0),
        name="tasks",
    )(*args)


def finish_own(data, acc):
    nblocks = data.shape[0] // 6
    return pl.pallas_call(
        lambda data_ref, acc_ref, out_ref: finish(data_ref, 0, acc_ref, out_ref),
        out_shape=jax.ShapeDtypeStruct((2, 3, nblocks, 128), F32),
        in_specs=[VMEM] * 2,
        out_specs=VMEM,
        compiler_params=params(16),
        name="finish_own",
    )(data, acc)


class Piece:
    def __init__(self, tags, array):
        self.tags, self.array = list(tags), array


def join(pieces):
    if len(pieces) == 1:
        return pieces[0]
    return Piece(sum([p.tags for p in pieces], []), jnp.concatenate([p.array for p in pieces], axis=0))


def swap(piece, bit, ndev):
    pairs = [(i, i ^ (1 << bit)) for i in range(ndev)]
    return Piece([t ^ (1 << bit) for t in piece.tags], lax.ppermute(piece.array, AXES, pairs))


def on_device(positions, direction, pair_local, pair_peer, pair_remote, pair_mask):
    npairs = pair_local.shape[0]
    ndev = lax.axis_size(AXES)
    me = lax.axis_index(AXES).astype(I32).reshape(1)
    slots = max(2, 2 * npairs // ndev)
    stride = -(-(slots + 2) // 8) * 8
    peer, local, remote = (a.reshape(1, npairs) for a in (pair_peer, pair_local, pair_remote))
    data = weave(positions, direction)
    send, keep, give = pack(ndev, slots, stride, me, peer, local, remote, pair_mask, data)
    groups = [list(range(core, ndev, 2)) for core in range(2)]
    came = lax.all_to_all(send, AXES, split_axis=0, concat_axis=0, axis_index_groups=groups, tiled=True)
    siblings = [(i, i ^ 1) for i in range(ndev)]
    sibling = lax.ppermute(data, AXES, siblings)
    got = lax.ppermute(give, AXES, siblings)

    bits = ndev.bit_length() - 1
    x, y = bits - 2, bits - 1
    early = Piece([0], data)
    for bit in range(bits - 3, 1, -1):
        early = join([early, swap(early, bit, ndev)])
    late = swap(early, 1, ndev)
    early_x, early_y = swap(early, x, ndev), swap(early, y, ndev)
    column = join([early, late])
    column.array, came = lax.optimization_barrier((column.array, came))
    late.array = column.array[early.array.shape[0] :]
    late_x, late_y = swap(late, x, ndev), swap(late, y, ndev)

    calls = [[column], [early_x, late_x, early_y, late_y]]
    lists = [sum([piece.tags for piece in call], []) for call in calls]
    lists.append([tag ^ (1 << x) ^ (1 << y) for tag in lists[0]])
    list_, where, masks, own = plan(slots, stride, lists, me, keep, got, came, data, sibling)
    run = functools.partial(tasks, list_=list_, where=where, mask=masks, came=came, own=own, sibling=sibling)

    def after(pieces, *arrays):
        held = lax.optimization_barrier(tuple(piece.array for piece in pieces) + arrays)
        return held[: len(pieces)], held[len(pieces) :]

    acc = run(0, blocks=[piece.array for piece in calls[0]], before=None, last=False)
    corner = [swap(early_y, x, ndev)]
    blocks, (acc,) = after(calls[1], acc)
    late_y.array = blocks[3]
    corner.append(swap(late_y, x, ndev))
    acc = run(1, blocks=blocks, before=acc, last=False)
    blocks, (acc,) = after(corner, acc)
    other, acc = run(2, blocks=blocks, before=acc, last=True)
    total = finish_own(data, acc) + lax.ppermute(other, AXES, siblings)
    return total[0], total[1]


def solution(mesh):
    blocked = P(None, AXES, None)
    in_specs = (blocked, blocked, P(AXES), P(AXES, None), P(AXES), P(AXES, None))
    return jax.shard_map(on_device, mesh=mesh, in_specs=in_specs, out_specs=(blocked, blocked), check_vma=False)
```

```python
import functools

import jax
import jax.numpy as jnp
import numpy as np
from jax import lax
from jax.experimental import pallas as pl
from jax.experimental.pallas import tpu as pltpu
from jax.sharding import PartitionSpec as P

AXES = ("dom", "brick")
F32, BF16, I32 = jnp.float32, jnp.bfloat16, jnp.int32
GROUP = 64
OWN, MASK = 1 << 12, 1 << 19
LOG_SCALE = 2.0 * 0.6931471805599453
SMEM = pl.BlockSpec(memory_space=pltpu.SMEM)
VMEM = pl.BlockSpec(memory_space=pltpu.VMEM)
HBM = pl.BlockSpec(memory_space=pltpu.HBM)
ANY = pl.BlockSpec(memory_space=pl.ANY)


def iota(shape, dim):
    return lax.broadcasted_iota(I32, shape, dim)


def params(mib):
    return pltpu.CompilerParams(vmem_limit_bytes=mib << 20)


def fetch(pairs, sems):
    copies = [pltpu.make_async_copy(src, dst, sems.at[i]) for i, (src, dst) in enumerate(pairs)]
    for copy in copies:
        copy.start()
    for copy in copies:
        copy.wait()


def weave_kernel(pos_hbm, dir_hbm, data_ref, pos_ref, dir_ref, sems):
    fetch([(pos_hbm, pos_ref), (dir_hbm, dir_ref)], sems)
    nblocks = pos_ref.shape[1]
    for c in range(3):
        data_ref[pl.ds(c, nblocks, stride=6), :] = pos_ref[c]
        data_ref[pl.ds(3 + c, nblocks, stride=6), :] = dir_ref[c]


def weave(positions, direction):
    nblocks = positions.shape[1]
    whole = pltpu.VMEM(positions.shape, F32)
    return pl.pallas_call(
        weave_kernel,
        out_shape=jax.ShapeDtypeStruct((nblocks * 6, 128), F32),
        in_specs=[HBM] * 2,
        out_specs=VMEM,
        scratch_shapes=[whole, whole, pltpu.SemaphoreType.DMA((2,))],
        compiler_params=params(60),
        name="weave",
    )(positions, direction)


def pack_kernel(
    ndev, slots, stride, me_ref, peer_hbm, local_hbm, remote_hbm, mask_hbm, data_hbm, send_ref, keep_ref, give_ref,
    peer_ref, local_ref, remote_ref, mask_ref, sems,
):
    fetch([(peer_hbm, peer_ref), (local_hbm, local_ref), (remote_hbm, remote_ref), (mask_hbm, mask_ref)], sems)
    npairs = peer_ref.shape[1]
    square = (npairs, npairs)
    rows, cols = iota(square, 0), iota(square, 1)

    def column(row):
        return jnp.sum(jnp.where(rows == cols, row, 0), axis=1, keepdims=True)

    peer = peer_ref[...]
    peer_col = column(peer)
    same = peer_col == peer
    rank = jnp.sum(jnp.where(same & (rows < cols), 1, 0), axis=0, keepdims=True)
    rank_col = jnp.sum(jnp.where(same & (cols < rows), 1, 0), axis=1, keepdims=True)
    local_col, remote_col = column(local_ref[...]), column(remote_ref[...])
    lane = iota((npairs, 128), 1)
    part, place = lane // slots, lane % slots
    value = jnp.where(part == 0, local_col, jnp.where(part == 1, remote_col, jnp.where(part == 2, 1, 0)))
    numbers = jnp.where(place == rank_col, value, 0).astype(F32).astype(BF16)
    mask = mask_ref[...].astype(F32).astype(BF16)
    slot = iota((ndev * stride, npairs), 0)

    def chunks(at):
        hot = jnp.where(slot == at * stride + rank, 1.0, 0.0).astype(BF16)
        hot_numbers = jnp.where(slot == at * stride + slots, 1.0, 0.0).astype(BF16)
        return jnp.dot(hot, mask, preferred_element_type=F32) + jnp.dot(hot_numbers, numbers, preferred_element_type=F32)

    send_ref[...] = chunks(peer)
    by_core = chunks(peer // 2 + ((peer ^ me_ref[0]) & 1) * (ndev // 2))
    keep_ref[...] = by_core[: ndev * stride // 2]
    give_ref[...] = by_core[ndev * stride // 2 :]


def pack(ndev, slots, stride, me, peer, local, remote, mask, data):
    row = pltpu.VMEM(peer.shape, I32)
    whole, half = (jax.ShapeDtypeStruct((ndev * stride // k, 128), F32) for k in (1, 2))
    return pl.pallas_call(
        functools.partial(pack_kernel, ndev, slots, stride),
        out_shape=(whole, half, half),
        in_specs=[SMEM] + [HBM] * 4 + [ANY],
        out_specs=(VMEM,) * 3,
        scratch_shapes=[row, row, row, pltpu.VMEM(mask.shape, I32), pltpu.SemaphoreType.DMA((4,))],
        compiler_params=params(60),
        name="pack",
    )(me, peer, local, remote, mask, data)


def load_block(ref, block):
    last = ref.shape[0] - 8
    start = block * 6
    d = ref[pl.ds(jnp.minimum(start, last), 8), :]
    return jnp.where(start > last, pltpu.roll(d, 6, 0), d)


def split(v):
    h = v.astype(BF16).astype(F32)
    e = v - h
    m = e.astype(BF16).astype(F32)
    return h, m, e - m


def products(d, h, m, row):
    both = h + m
    return both * jnp.where(row < 3, both, pltpu.roll(both, 3, 0))


def other_features(d, row):
    h, m, l = split(d)
    vh, vm, vl = split(products(d, h, m, row))
    hm = jnp.concatenate([h, m], 0).astype(BF16)
    vhm = jnp.concatenate([vh, vm], 0).astype(BF16)
    vlo = jnp.concatenate([vl, jnp.ones_like(d)], 0).astype(BF16)
    first = jnp.where(row < 6, h, jnp.where(row == 6, 1.0, pltpu.roll(l, 7, 0)))
    second = jnp.where(row < 6, m, pltpu.roll(l, 5, 0))
    return jnp.concatenate([hm, hm, vhm, vlo], 0), jnp.concatenate([first, second], 0)


def own_features(d, row):
    d = jnp.where(row < 6, d, 0.0)
    h, m, _ = split(d)
    v = products(d, h, m, row)
    total = v + pltpu.roll(v, 7, 0) + pltpu.roll(v, 6, 0)

    def parts(one_row):
        ph, pm, pl_ = split(jnp.broadcast_to(one_row, d.shape))
        return jnp.where(row == 0, ph, jnp.where(row == 1, pm, jnp.where(row == 2, pl_, 0.0)))

    def cross(a):
        return jnp.where(row < 3, -pltpu.roll(a, 5, 0), jnp.where(row < 6, -pltpu.roll(a, 3, 0), 0.0))

    hs, ms = jnp.where(row < 3, -2.0 * h, 0.0), jnp.where(row < 3, -2.0 * m, 0.0)
    hq, mq = cross(h), cross(m)
    low = jnp.where(row < 3, 1.0, 0.0)
    high = jnp.where((row >= 3) & (row < 6), 1.0, 0.0)
    for_s = jnp.concatenate([hs, ms, ms, hs, low, low, low, parts(total[0:1] + 0.1)], 0)
    for_q = jnp.concatenate([hq, mq, mq, hq, high, high, high, parts(total[3:4])], 0)
    return jnp.concatenate([for_s, for_q], 1).astype(BF16)


def plan_kernel(
    slots, stride, sizes, me_ref, order_ref, table_ref, keep_ref, got_ref, came_ref, data_ref, sibling_ref,
    list_ref, where_ref, masks_ref, own_ref, code_vmem, code_smem, sem,
):
    chips = keep_ref.shape[0] // stride
    nblocks = own_ref.shape[0] // 2
    me = me_ref[0]
    mine, core = me // 2, me % 2
    lane = iota((chips, 128), 1)
    chip = iota((chips, 128), 0)
    rel = iota((chips, chips), 0) ^ mine
    first_block = jnp.sum(jnp.where(iota((chips, chips), 1) == rel, table_ref[...], 0), axis=1, keepdims=True)

    code = jnp.zeros((chips, 128), I32)
    sides = (
        (keep_ref[pl.ds(slots, chips, stride=stride), :], True, 0, chip * stride),
        (got_ref[pl.ds(slots, chips, stride=stride), :], True, nblocks, (chips + chip) * stride),
        (came_ref[pl.ds(slots, chips, stride=2 * stride), :], False, core * nblocks, (2 * chips + 2 * chip) * stride),
        (came_ref[pl.ds(slots + stride, chips, stride=2 * stride), :], False, (1 - core) * nblocks, (2 * chips + 2 * chip + 1) * stride),
    )
    for i, (numbers, left, base, mask) in enumerate(sides):
        numbers = numbers.astype(I32)
        second = pltpu.roll(numbers, 128 - slots, 1)
        used = jnp.where((lane >= 2 * slots) & (lane < 3 * slots), numbers, 0)
        own, other = (numbers, second) if left else (second, numbers)
        part = jnp.where(lane < slots, (first_block + other) + (own + base) * OWN + (mask + lane) * MASK, 0)
        code += pltpu.roll(part, i * slots, 1) if i else part
        code += jnp.where(lane == len(sides) * slots + i, jnp.sum(used, axis=1, keepdims=True), 0)
    code_vmem[...] = code
    copy = pltpu.make_async_copy(code_vmem, code_smem, sem)
    copy.start()
    masks_ref[: chips * stride, :] = keep_ref[...]
    masks_ref[chips * stride :, :] = got_ref[...]
    row = iota((8, 128), 0)

    def feature(i, _):
        for u in range(4):
            own_ref[i * 4 + u] = own_features(load_block(data_ref, i * 4 + u), row)
            own_ref[nblocks + i * 4 + u] = own_features(load_block(sibling_ref, i * 4 + u), row)
        return 0

    lax.fori_loop(0, nblocks // 4, feature, 0)
    copy.wait()
    start, done = jnp.int32(0), 0
    for k, size in enumerate(sizes):

        def fill(i, at):
            p = order_ref[i] ^ mine
            counts = [code_smem[p, len(sides) * slots + side] for side in range(len(sides))]
            for side, count in enumerate(counts):
                held = [code_smem[p, side * slots + r] for r in range(slots)]
                for r in range(slots):
                    list_ref[at + r] = held[r]
                at = at + count
            return at

        end = lax.fori_loop(done, done + size, fill, start)
        done += size
        for r in range(GROUP):
            list_ref[end + r] = (2 * chips * stride + slots + 1) * MASK
        where_ref[2 * k] = start
        where_ref[2 * k + 1] = end - start
        start = end + GROUP


def plan(slots, stride, lists, me, keep, got, came, data, sibling):
    chips, nblocks = keep.shape[0] // stride, data.shape[0] // 6
    order = np.array(sum(lists, []), np.int32) // 2
    table = np.zeros((1, chips), np.int32)
    for tags in lists:
        table[0, np.array(tags) // 2] = np.arange(len(tags)) * nblocks
    length = 4 * chips * slots + len(lists) * GROUP + slots + GROUP
    return pl.pallas_call(
        functools.partial(plan_kernel, slots, stride, [len(tags) for tags in lists]),
        out_shape=(
            jax.ShapeDtypeStruct((length,), I32),
            jax.ShapeDtypeStruct((2 * len(lists),), I32),
            jax.ShapeDtypeStruct((2 * chips * stride, 128), F32),
            jax.ShapeDtypeStruct((2 * nblocks, 64, 256), BF16),
        ),
        in_specs=[SMEM] * 2 + [VMEM] * 6,
        out_specs=(SMEM, SMEM, VMEM, VMEM),
        scratch_shapes=[pltpu.VMEM((chips, 128), I32), pltpu.SMEM((chips, 128), I32), pltpu.SemaphoreType.DMA],
        compiler_params=params(24),
        name="plan",
    )(me, jnp.asarray(order), jnp.asarray(table), keep, got, came, data, sibling)


def halves(c):
    h = c.astype(BF16)
    return h, (c - h.astype(F32)).astype(BF16)


def prepare(codes, block_ref, came_ref, nleft, k_ref, f_ref):
    row = iota((8, 128), 0)
    for g, code in enumerate(codes):
        d = load_block(block_ref, code % OWN)
        left, sums = other_features(d, row)
        place = code // MASK - nleft
        mask = jnp.where(place < 0, 1.0, came_ref[pl.ds(jnp.maximum(place, 0), 1), :])
        f_ref[g] = (sums * mask).astype(BF16)
        k_ref[g] = left.T


def accumulate(codes, own_ref, mask_ref, acc_ref, k_ref, f_ref, base=0):
    nleft = mask_ref.shape[0]
    outs = []
    for g, code in enumerate(codes):
        own = code // OWN % (MASK // OWN)
        both = jnp.dot(k_ref[base + g], own_ref[own], preferred_element_type=F32)
        s = jnp.minimum(both[:, :128], 1.0)
        gap = s - 1.0
        log = LOG_SCALE * jnp.log2(s)
        ratio = gap * pl.reciprocal(s, approx=True)
        one = gap * (log + ratio)
        two = ((ratio - 4.0) * ratio - log) * both[:, 128:]
        one_h, one_l = halves(one)
        two_h, two_l = halves(two)
        weights = jnp.concatenate([jnp.concatenate([one_h, two_h], 1), jnp.concatenate([one_l, two_l], 1)], 0)
        f = f_ref[base + g]
        out = jnp.dot(jnp.concatenate([f, f], 1), weights, preferred_element_type=F32)
        place = code // MASK
        mask = mask_ref[pl.ds(jnp.minimum(place, nleft - 1), 1), :]
        mask = jnp.where(place < nleft, mask, 1.0)
        outs.append((own, out * jnp.concatenate([mask, mask], 1)))
    for own, out in outs:
        acc_ref[own] += out


def finish(data_ref, first, acc_ref, out_ref):
    nblocks = out_ref.shape[2]
    row = iota((8, 128), 0)

    def block(b):
        d = load_block(data_ref, b)
        acc = acc_ref[first + b]

        def sums(a):
            first, second = a[0:8], a[8:16]
            total = first + second
            low = jnp.where(row == 0, pltpu.roll(first, 1, 0), jnp.where(row < 3, pltpu.roll(second, 3, 0), 0.0))
            return first[6:7], total + low

        n_one, y_one = sums(acc[:, :128] * -0.01)
        n_two, y_two = sums(acc[:, 128:] * 0.02)
        a = d * n_one - y_one
        c = d * n_two - y_two + pltpu.roll(a, 5, 0)
        for k in range(3):
            out_ref[0, k, pl.ds(b, 1), :] = a[k : k + 1]
            out_ref[1, k, pl.ds(b, 1), :] = c[k : k + 1]

    def some(i, _):
        for u in range(16):
            block(i * 16 + u)
        return 0

    lax.fori_loop(0, nblocks // 16, some, 0)


def task_kernel(which, count, first, last, *refs):
    list_ref, where_ref, mask_ref, came_ref, own_ref, sibling_ref = refs[:6]
    nleft = mask_ref.shape[0]
    arrays, refs = refs[6 : 6 + count], refs[6 + count :]
    if not first:
        before_ref, refs = refs[0], refs[1:]
    if last:
        other_ref, refs = refs[0], refs[1:]
    acc_ref, k_ref, f_ref = refs[:3]
    if count == 1:
        block_ref = arrays[0]
    else:
        block_ref, sems = refs[-2:]
        rows = arrays[0].shape[0]
        copies = [
            pltpu.make_async_copy(array, block_ref.at[pl.ds(i * rows, rows), :], sems.at[i]) for i, array in enumerate(arrays)
        ]
        for copy in copies:
            copy.start()
    if first:
        acc_ref[...] = jnp.zeros_like(acc_ref)
    else:
        acc_ref[...] = before_ref[...]
    if count > 1:
        for copy in copies:
            copy.wait()
    start, total = where_ref[2 * which], where_ref[2 * which + 1]
    half, quarter = GROUP // 2, GROUP // 4
    rest = total % GROUP
    groups = total // GROUP + jnp.where(rest > half + quarter, 1, 0)
    rest = jnp.maximum(total - groups * GROUP, 0)
    skip = jnp.where(rest > quarter, half, 0)

    def codes(first, size):
        return [list_ref[start + first + g] for g in range(size)]

    def get_ready(i):
        first = jnp.minimum(i, jnp.maximum(total - 1, 0) // GROUP) * GROUP
        prepare(codes(first, GROUP), block_ref, came_ref, nleft, k_ref, f_ref)

    def add(first, size, base=0):
        accumulate(codes(first, size), own_ref, mask_ref, acc_ref, k_ref, f_ref, base)

    get_ready(0)

    def step(i, _):
        add(i * GROUP, GROUP)
        get_ready(i + 1)
        return 0

    lax.fori_loop(0, groups, step, 0)

    @pl.when(rest > quarter)
    def _():
        add(groups * GROUP, half)

    @pl.when(rest > skip)
    def _():
        add(groups * GROUP + skip, quarter, skip)

    if last:
        finish(sibling_ref, other_ref.shape[2], acc_ref, other_ref)


def tasks(which, list_, where, mask, came, own, sibling, blocks, before, last):
    nblocks = own.shape[0] // 2
    acc = jax.ShapeDtypeStruct((2 * nblocks, 16, 256), F32)
    out = jax.ShapeDtypeStruct((2, 3, nblocks, 128), F32)
    first = before is None
    count = len(blocks)
    scratch = [pltpu.VMEM((GROUP, 128, 64), BF16), pltpu.VMEM((GROUP, 16, 128), BF16)]
    if count > 1:
        scratch += [pltpu.VMEM((count * blocks[0].shape[0], 128), F32), pltpu.SemaphoreType.DMA((count,))]
    args = [list_, where, mask, came, own, sibling, *blocks] + ([] if first else [before])
    size = sum(b.size for b in blocks) * 4
    return pl.pallas_call(
        functools.partial(task_kernel, which, count, first, last),
        out_shape=(out, acc) if last else acc,
        in_specs=[SMEM, SMEM] + [VMEM] * 4 + [VMEM if count == 1 else ANY] * count + ([] if first else [VMEM]),
        out_specs=(VMEM, VMEM) if last else VMEM,
        scratch_shapes=scratch,
        compiler_params=params(16),
        cost_estimate=pl.CostEstimate(flops=size * 2000, bytes_accessed=size * 3, transcendentals=0),
        name="tasks",
    )(*args)


def finish_own(data, acc):
    nblocks = data.shape[0] // 6
    return pl.pallas_call(
        lambda data_ref, acc_ref, out_ref: finish(data_ref, 0, acc_ref, out_ref),
        out_shape=jax.ShapeDtypeStruct((2, 3, nblocks, 128), F32),
        in_specs=[VMEM] * 2,
        out_specs=VMEM,
        compiler_params=params(16),
        name="finish_own",
    )(data, acc)


class Piece:
    def __init__(self, tags, array):
        self.tags, self.array = list(tags), array


def join(pieces):
    if len(pieces) == 1:
        return pieces[0]
    return Piece(sum([p.tags for p in pieces], []), jnp.concatenate([p.array for p in pieces], axis=0))


def swap(piece, bit, ndev):
    pairs = [(i, i ^ (1 << bit)) for i in range(ndev)]
    return Piece([t ^ (1 << bit) for t in piece.tags], lax.ppermute(piece.array, AXES, pairs))


def on_device(positions, direction, pair_local, pair_peer, pair_remote, pair_mask):
    npairs = pair_local.shape[0]
    ndev = lax.axis_size(AXES)
    me = lax.axis_index(AXES).astype(I32).reshape(1)
    slots = max(2, 2 * npairs // ndev)
    stride = -(-(slots + 2) // 8) * 8
    peer, local, remote = (a.reshape(1, npairs) for a in (pair_peer, pair_local, pair_remote))
    data = weave(positions, direction)
    send, keep, give = pack(ndev, slots, stride, me, peer, local, remote, pair_mask, data)
    groups = [list(range(core, ndev, 2)) for core in range(2)]
    came = lax.all_to_all(send, AXES, split_axis=0, concat_axis=0, axis_index_groups=groups, tiled=True)
    siblings = [(i, i ^ 1) for i in range(ndev)]
    sibling = lax.ppermute(data, AXES, siblings)
    got = lax.ppermute(give, AXES, siblings)

    bits = ndev.bit_length() - 1
    x, y = bits - 2, bits - 1
    early = Piece([0], data)
    for bit in range(bits - 3, 1, -1):
        early = join([early, swap(early, bit, ndev)])
    late = swap(early, 1, ndev)
    early_x, early_y = swap(early, x, ndev), swap(early, y, ndev)
    column = join([early, late])
    column.array, came = lax.optimization_barrier((column.array, came))
    late.array = column.array[early.array.shape[0] :]
    late_x, late_y = swap(late, x, ndev), swap(late, y, ndev)

    calls = [[column], [early_x, late_x, early_y, late_y]]
    lists = [sum([piece.tags for piece in call], []) for call in calls]
    lists.append([tag ^ (1 << x) ^ (1 << y) for tag in lists[0]])
    list_, where, masks, own = plan(slots, stride, lists, me, keep, got, came, data, sibling)
    run = functools.partial(tasks, list_=list_, where=where, mask=masks, came=came, own=own, sibling=sibling)

    def after(pieces, *arrays):
        held = lax.optimization_barrier(tuple(piece.array for piece in pieces) + arrays)
        return held[: len(pieces)], held[len(pieces) :]

    acc = run(0, blocks=[piece.array for piece in calls[0]], before=None, last=False)
    corner = [swap(early_y, x, ndev)]
    blocks, (acc,) = after(calls[1], acc)
    late_y.array = blocks[3]
    corner.append(swap(late_y, x, ndev))
    acc = run(1, blocks=blocks, before=acc, last=False)
    blocks, (acc,) = after(corner, acc)
    other, acc = run(2, blocks=blocks, before=acc, last=True)
    total = finish_own(data, acc) + lax.ppermute(other, AXES, siblings)
    return total[0], total[1]


def solution(mesh):
    blocked = P(None, AXES, None)
    in_specs = (blocked, blocked, P(AXES), P(AXES, None), P(AXES), P(AXES, None))
    return jax.shard_map(on_device, mesh=mesh, in_specs=in_specs, out_specs=(blocked, blocked), check_vma=False)
```
